256 devices in a mesh: row: 16 (over x, z_hi, core), col: 16 (over y, z_lo).
Axes of the slice: x: 4, y: 4, z: 8 (z_hi: 2, z_lo: 4; z = z_hi * 4 + z_lo), core: 2. Of those that a mesh axis runs over, the one named last changes fastest.
Arguments:
- tokens: bfloat16 [768, 6144], P('col', 'row'), may hold values from -6 to 6
- gate_weight: bfloat16 [6144, 14336], P('row', 'col'), may hold values from -0.078125 to 0.078125
- up_weight: bfloat16 [6144, 14336], P('row', 'col'), may hold values from -0.078125 to 0.078125
- down_weight: bfloat16 [14336, 6144], P('col', 'row'), may hold values from -0.046875 to 0.046875
- cotangent: bfloat16 [768, 6144], P('col', 'row'), may hold values from -6 to 6
Outputs:
- output: bfloat16 [768, 6144], P('col', 'row')
- grad_input: bfloat16 [768, 6144], P('col', 'row')
- grad_gate: float32 [6144, 14336], P('row', 'col')
- grad_up: float32 [6144, 14336], P('row', 'col')
- grad_down: float32 [14336, 6144], P('col', 'row')
The draws below stay inside these ranges and needn't reach their ends.
All inputs are finite; a program needn't handle non-finite values.
Results may differ from the reference program's by a relative error of at most 0.0049.
Values may be sent and summed in bfloat16 or wider, within the bound.
A program may use at most 64 MiB of HBM per device.

```python
import jax
import jax.numpy as jnp

D = 6144
FF = 14336
TOKENS = 768


def shard_levels(key, shape, pieces, least, high):
    level = 1.0
    for position, shards_of in pieces:
        steps = jax.random.uniform(jax.random.fold_in(jax.random.fold_in(key, 6), position), (shards_of,), jnp.float32, least / len(pieces), high / len(pieces))
        level = level * jnp.repeat(jnp.exp(steps), shape[position] // shards_of).reshape((-1,) + (1,) * (len(shape) - 1 - position))
    return level


def centred(rng, extent, scale, most, shards=(), held_as=jnp.bfloat16):
    array = scale * jax.random.normal(rng, extent, jnp.float32)
    if shards:
        array = array * shard_levels(rng, extent, shards, -0.22, 0.18)
    return jnp.clip(array, -most, most).astype(held_as)


def setup_inputs(seed: int = 0) -> dict:
    arg_keys = jax.random.split(jax.random.key(seed), 6)
    tokens = centred(arg_keys[0], (TOKENS, D), 1.0, 6.0, ((0, 16), (1, 16)))
    gate_weight = centred(arg_keys[1], (D, FF), D ** -0.5, 0.078125, ((0, 16), (1, 16)))
    up_weight = centred(arg_keys[2], (D, FF), D ** -0.5, 0.078125, ((0, 16), (1, 16)))
    down_weight = centred(arg_keys[3], (FF, D), FF ** -0.5, 0.046875, ((0, 16), (1, 16)))
    cotangent = centred(arg_keys[4], (TOKENS, D), 1.0, 6.0, ((0, 16), (1, 16)))
    return dict(tokens=tokens, gate_weight=gate_weight, up_weight=up_weight, down_weight=down_weight, cotangent=cotangent)


def reference(tokens, gate_weight, up_weight, down_weight, cotangent):
    scale = TOKENS ** -0.5
    gate = jnp.dot(tokens, gate_weight, preferred_element_type=jnp.float32)
    up = jnp.dot(tokens, up_weight, preferred_element_type=jnp.float32)
    sig = jax.nn.sigmoid(gate)
    hidden = (gate * sig * up).astype(jnp.bfloat16)
    output = jnp.dot(hidden, down_weight, preferred_element_type=jnp.float32).astype(jnp.bfloat16)
    d_hidden = jnp.dot(cotangent, down_weight.T, preferred_element_type=jnp.float32)
    grad_down = jnp.dot(hidden.T, cotangent, preferred_element_type=jnp.float32) * scale
    d_up = (d_hidden * gate * sig).astype(jnp.bfloat16)
    d_gate = (d_hidden * up * sig * (1.0 + gate * (1.0 - sig))).astype(jnp.bfloat16)
    grad_gate = jnp.dot(tokens.T, d_gate, preferred_element_type=jnp.float32) * scale
    grad_up = jnp.dot(tokens.T, d_up, preferred_element_type=jnp.float32) * scale
    grad_input = (jnp.dot(d_gate, gate_weight.T, preferred_element_type=jnp.float32)
                  + jnp.dot(d_up, up_weight.T, preferred_element_type=jnp.float32)).astype(jnp.bfloat16)
    return output, grad_input, grad_gate, grad_up, grad_down
```

```python
import functools

import jax
import jax.numpy as jnp
from jax import lax
from jax.experimental import pallas as pl
from jax.experimental.pallas import tpu as pltpu
from jax.sharding import PartitionSpec as P

STAGES = 3
BF16 = jnp.bfloat16
F32 = jnp.float32


def dot(a, b, dims):
    return lax.dot_general(a, b, (dims, ((), ())), preferred_element_type=F32)


def kernel(
    scale,
    tok_in, wg_in, wu_in, wd_in, cot_in,
    out_ref, gin_ref, gg_hbm, gu_hbm, gd_hbm,
    panel, other, wg, wu, wd,
    part, part_own, rs_x, zs, zr, hid,
    oparts, oparts_own, rs_y, zout, rs_z,
    gg, gu, gd,
    load_sem, wsend, wrecv,
    azs, azr, ays, ayr, afs, afr,
    xrs, xrr, z4s, z4r, xas, xar, hfs, hfr,
    yrs, yrr, zrs, zrr, store_sem,
):
    row = lax.axis_index("row")
    col = lax.axis_index("col")
    x = row // 4
    zh = (row // 2) % 2
    k = row % 2
    y = col // 4
    zl = col % 4

    def at(dx=0, dz4=0, dk=0, dy=0, dz=0):
        xx = (x + dx) % 4
        zz = (zh + dz4) % 2
        kk = (k + dk) % 2
        yy = (y + dy) % 4
        ll = (zl + dz) % 4
        return {"row": xx * 4 + zz * 2 + kk, "col": yy * 4 + ll}

    sends = []

    def remote(src, dst, ssem, rsem, device):
        copy = pltpu.make_async_remote_copy(
            src_ref=src, dst_ref=dst, send_sem=ssem, recv_sem=rsem,
            device_id=device, device_id_type=pl.DeviceIdType.MESH,
        )
        copy.start()
        sends.append(copy)
        return copy

    loads = []
    ins = (tok_in, cot_in)
    for tc in range(2):
        for j in range(STAGES):
            loads.append(pltpu.make_async_copy(
                ins[tc].at[pl.ds(16 * j, 16)],
                panel.at[j, tc, zl // 2, y, zl % 2],
                load_sem.at[tc * STAGES + j],
            ))
    for i, (src, dst) in enumerate(((wg_in, wg), (wu_in, wu), (wd_in, wd))):
        loads.append(pltpu.make_async_copy(src, dst.at[0], load_sem.at[2 * STAGES + i]))
    for load in loads:
        load.start()

    barrier = pltpu.get_barrier_semaphore()
    peers = [at(dk=1), at(dz4=1)]
    peers += [at(dx=d) for d in (1, 2, 3)]
    peers += [at(dy=d) for d in (1, 2, 3)]
    peers += [at(dz=d) for d in (1, 2, 3)]
    for peer in peers:
        pl.semaphore_signal(barrier, inc=1, device_id=peer, device_id_type=pl.DeviceIdType.MESH)
    pl.semaphore_wait(barrier, len(peers))

    az = {}
    for j in range(STAGES):
        for tc in range(2):
            for d in (1, 2, 3):
                az[j, tc, d] = remote(
                    ins[tc].at[pl.ds(16 * j, 16)],
                    panel.at[j, tc, zl // 2, y, zl % 2],
                    azs.at[j, tc, d - 1], azr.at[j, tc, d - 1], at(dz=d),
                )
    wx = []
    for i, (src, dst) in enumerate(((wg_in, wg), (wu_in, wu), (wd_in, wd))):
        wx.append(remote(src, dst.at[1], wsend.at[i], wrecv.at[i], at(dk=1)))

    ay, af = {}, {}

    def gather_y(j):
        for tc in range(2):
            loads[tc * STAGES + j].wait()
            for d in (1, 2, 3):
                az[j, tc, d].wait_recv()
            for d in (1, 2, 3):
                ay[j, tc, d] = remote(
                    panel.at[j, tc, :, y], panel.at[j, tc, :, y],
                    ays.at[j, tc, d - 1], ayr.at[j, tc, d - 1], at(dy=d),
                )

    def forward_core(j):
        for tc in range(2):
            for d in (1, 2, 3):
                ay[j, tc, d].wait_recv()
            af[j, tc] = remote(
                panel.at[j, tc, 1 - k], other.at[j, tc],
                afs.at[j, tc], afr.at[j, tc], at(dk=1),
            )

    xr = {}

    def partials(j):
        for a in range(3):
            tc = 0 if a < 2 else 1
            if a != 1:
                af[j, tc].wait_recv()
            if j == 0:
                loads[2 * STAGES + a].wait()
                wx[a].wait_recv()
            lhs0 = panel[j, tc, k].reshape(128, 384)
            lhs1 = other[j, tc].reshape(128, 384)
            w = (wg, wu, wd)[a]
            if a < 2:
                res = dot(lhs0, w[0], ((1,), (0,))) + dot(lhs1, w[1], ((1,), (0,)))
            else:
                res = dot(lhs0, w[0], ((1,), (1,))) + dot(lhs1, w[1], ((1,), (1,)))
            part_own[j, a] = res.reshape(4, 32, 896)
            part[j, a] = res.astype(BF16).reshape(4, 32, 896)
            for d in (2, 1, 3):
                xr[j, a, d] = remote(
                    part.at[j, a, (x + d) % 4], rs_x.at[j, a, d - 1],
                    xrs.at[j, a, d - 1], xrr.at[j, a, d - 1], at(dx=d),
                )

    z4 = {}

    def sum_x(j):
        for a in range(3):
            for d in (1, 2, 3):
                xr[j, a, d].wait_recv()
            total = part_own[j, a, x]
            for d in (1, 2, 3):
                total = total + rs_x[j, a, d - 1].astype(F32)
            part_own[j, a, x] = total
            zs[j, a] = total.astype(BF16)
            z4[j, a] = remote(
                zs.at[j, a], zr.at[j, a], z4s.at[j, a], z4r.at[j, a], at(dz4=1),
            )

    xa, hf = {}, {}

    def spread(j, a, value):
        hid[j, a, k, x] = value.astype(BF16)
        for d in (2, 1, 3):
            xa[j, a, d] = remote(
                hid.at[j, a, k, x], hid.at[j, a, k, x],
                xas.at[j, a, d - 1], xar.at[j, a, d - 1], at(dx=d),
            )

    def middle(j):
        z4[j, 0].wait_recv()
        z4[j, 1].wait_recv()
        gate = part_own[j, 0, x] + zr[j, 0].astype(F32)
        up = part_own[j, 1, x] + zr[j, 1].astype(F32)
        sig = jax.nn.sigmoid(gate)
        spread(j, 0, gate * sig * up)
        z4[j, 2].wait_recv()
        d_hidden = part_own[j, 2, x] + zr[j, 2].astype(F32)
        spread(j, 1, d_hidden * up * sig * (1.0 + gate * (1.0 - sig)))
        spread(j, 2, d_hidden * gate * sig)

    def forward_hidden(j):
        for a in range(3):
            for d in (1, 2, 3):
                xa[j, a, d].wait_recv()
            hf[j, a] = remote(
                hid.at[j, a, k], hid.at[j, a, k], hfs.at[j, a], hfr.at[j, a], at(dk=1),
            )

    yr = {}

    def send_y(j, b, res):
        res = res.reshape(2, 4, 32, 384)
        oparts_own[j, b] = res
        oparts[j, b] = res.astype(BF16)
        for d in (2, 1, 3):
            yr[j, b, d] = remote(
                oparts.at[j, b, :, (y + d) % 4], rs_y.at[j, b, d - 1],
                yrs.at[j, b, d - 1], yrr.at[j, b, d - 1], at(dy=d),
            )

    def back(j):
        for a in range(3):
            hf[j, a].wait_recv()
        h = hid[j, 0].reshape(256, 896)
        dg = hid[j, 1].reshape(256, 896)
        du = hid[j, 2].reshape(256, 896)
        send_y(j, 0, dot(h, wd[0], ((1,), (0,))))
        send_y(j, 1, dot(dg, wg[0], ((1,), (1,))) + dot(du, wu[0], ((1,), (1,))))

    def grads(j):
        h = hid[j, 0].reshape(256, 896)
        dg = hid[j, 1].reshape(256, 896)
        du = hid[j, 2].reshape(256, 896)
        tok = panel[j, 0].reshape(256, 384)
        cot = panel[j, 1].reshape(256, 384)
        for acc, l, r in ((gg, tok, dg), (gu, tok, du), (gd, h, cot)):
            term = dot(l, r, ((0,), (0,)))
            if j > 0:
                term = acc[...] + term
            if j == STAGES - 1:
                term = term * scale
            acc[...] = term

    zrc = {}

    def sum_y(j):
        for b in range(2):
            for d in (1, 2, 3):
                yr[j, b, d].wait_recv()
            total = oparts_own[j, b, :, y]
            for d in (1, 2, 3):
                total = total + rs_y[j, b, d - 1].astype(F32)
            oparts_own[j, b, :, y] = total
            zout[j, b] = total.astype(zout.dtype).reshape(4, 16, 384)
            for d in (1, 2, 3):
                zrc[j, b, d] = remote(
                    zout.at[j, b, (zl + d) % 4], rs_z.at[j, b, d - 1],
                    zrs.at[j, b, d - 1], zrr.at[j, b, d - 1], at(dz=d),
                )

    def finish(j):
        for b in range(2):
            for d in (1, 2, 3):
                zrc[j, b, d].wait_recv()
            total = oparts_own[j, b, zl // 2, y, pl.ds(pl.multiple_of(zl % 2 * 16, 16), 16)]
            for d in (1, 2, 3):
                total = total + rs_z[j, b, d - 1].astype(F32)
            (out_ref, gin_ref)[b][pl.ds(16 * j, 16)] = total.astype(BF16)

    gather_y(0)
    gather_y(1)
    forward_core(0)
    gather_y(2)
    partials(0)
    forward_core(1)
    partials(1)
    forward_core(2)
    partials(2)
    sum_x(0)
    sum_x(1)
    middle(0)
    sum_x(2)
    middle(1)
    forward_hidden(0)
    middle(2)
    back(0)
    grads(0)
    forward_hidden(1)
    back(1)
    grads(1)
    sum_y(0)
    forward_hidden(2)
    back(2)
    sum_y(1)
    finish(0)
    grads(2)
    stores = []
    for i, (src, dst) in enumerate(((gg, gg_hbm), (gu, gu_hbm), (gd, gd_hbm))):
        store = pltpu.make_async_copy(src, dst, store_sem.at[i])
        store.start()
        stores.append(store)
    sum_y(2)
    finish(1)
    finish(2)
    for store in stores:
        store.wait()
    for copy in sends:
        copy.wait_send()


def body(tokens, gate_weight, up_weight, down_weight, cotangent):
    total_tokens = tokens.shape[0] * lax.axis_size("col")
    scale = total_tokens ** (-0.5)
    vmem = pl.BlockSpec(memory_space=pltpu.VMEM)
    hbm = pl.BlockSpec(memory_space=pl.ANY)
    S = STAGES
    sem = pltpu.SemaphoreType.DMA
    scratch = [
        pltpu.VMEM((S, 2, 2, 4, 2, 16, 384), BF16),
        pltpu.VMEM((S, 2, 4, 2, 16, 384), BF16),
        pltpu.VMEM((2, 384, 896), BF16),
        pltpu.VMEM((2, 384, 896), BF16),
        pltpu.VMEM((2, 896, 384), BF16),
        pltpu.VMEM((S, 3, 4, 32, 896), BF16),
        pltpu.VMEM((S, 3, 4, 32, 896), F32),
        pltpu.VMEM((S, 3, 3, 32, 896), BF16),
        pltpu.VMEM((S, 3, 32, 896), BF16),
        pltpu.VMEM((S, 3, 32, 896), BF16),
        pltpu.VMEM((S, 3, 2, 4, 32, 896), BF16),
        pltpu.VMEM((S, 2, 2, 4, 32, 384), BF16),
        pltpu.VMEM((S, 2, 2, 4, 32, 384), F32),
        pltpu.VMEM((S, 2, 3, 2, 32, 384), BF16),
        pltpu.VMEM((S, 2, 4, 16, 384), BF16),
        pltpu.VMEM((S, 2, 3, 16, 384), BF16),
        pltpu.VMEM((384, 896), F32),
        pltpu.VMEM((384, 896), F32),
        pltpu.VMEM((896, 384), F32),
        sem((2 * S + 3,)), sem((3,)), sem((3,)),
        sem((S, 2, 3)), sem((S, 2, 3)), sem((S, 2, 3)), sem((S, 2, 3)), sem((S, 2)), sem((S, 2)),
        sem((S, 3, 3)), sem((S, 3, 3)), sem((S, 3)), sem((S, 3)),
        sem((S, 3, 3)), sem((S, 3, 3)), sem((S, 3)), sem((S, 3)),
        sem((S, 2, 3)), sem((S, 2, 3)), sem((S, 2, 3)), sem((S, 2, 3)), sem((3,)),
    ]
    return pl.pallas_call(
        functools.partial(kernel, scale),
        out_shape=(
            jax.ShapeDtypeStruct((48, 384), BF16),
            jax.ShapeDtypeStruct((48, 384), BF16),
            jax.ShapeDtypeStruct((384, 896), F32),
            jax.ShapeDtypeStruct((384, 896), F32),
            jax.ShapeDtypeStruct((896, 384), F32),
        ),
        in_specs=[hbm] * 5,
        out_specs=(vmem, vmem, hbm, hbm, hbm),
        scratch_shapes=scratch,
        compiler_params=pltpu.CompilerParams(
            collective_id=0, has_side_effects=True, vmem_limit_bytes=56 * 1024 * 1024,
        ),
        cost_estimate=pl.CostEstimate(
            flops=2 * 9 * 768 * 384 * 896, bytes_accessed=8 * 1024 * 1024, transcendentals=0,
        ),
        name="ffn",
    )(tokens, gate_weight, up_weight, down_weight, cotangent)


def solution(mesh):
    return jax.shard_map(
        body,
        mesh=mesh,
        in_specs=(
            P("col", "row"),
            P("row", "col"),
            P("row", "col"),
            P("col", "row"),
            P("col", "row"),
        ),
        out_specs=(
            P("col", "row"),
            P("col", "row"),
            P("row", "col"),
            P("row", "col"),
            P("col", "row"),
        ),
        check_vma=False,
    )
```

```python
import functools

import jax
import jax.numpy as jnp
from jax import lax
from jax.experimental import pallas as pl
from jax.experimental.pallas import tpu as pltpu
from jax.sharding import PartitionSpec as P

STAGES = 3
BF16 = jnp.bfloat16
F32 = jnp.float32


def dot(a, b, dims):
    return lax.dot_general(a, b, (dims, ((), ())), preferred_element_type=F32)


def kernel(
    scale,
    tok_in, wg_in, wu_in, wd_in, cot_in,
    out_any, gin_any, gg_any, gu_any, gd_any,
    panel, other, wg, wu, wd,
    part, part_own, rs_x, zs, zr, hid,
    oparts, oparts_own, rs_y, zout, rs_z,
    out_ref, gin_ref, big, gd,
    load_sem, wsend, wrecv,
    azs, azr, azr0, ats, atr, ays, ayr, afs, afr,
    xrs, xrr, z4s, z4r, xas, xar, xbr, hfs, hfr,
    yrs, yrr, zrs, zrr, store_sem,
):
    row = lax.axis_index("row")
    col = lax.axis_index("col")
    x = row // 4
    zh = (row // 2) % 2
    k = row % 2
    y = col // 4
    zl = col % 4

    def at(dx=0, dz4=0, dk=0, dy=0, dz=0):
        xx = (x + dx) % 4
        zz = (zh + dz4) % 2
        kk = (k + dk) % 2
        yy = (y + dy) % 4
        ll = (zl + dz) % 4
        return {"row": xx * 4 + zz * 2 + kk, "col": yy * 4 + ll}

    gg, gu = big.at[0], big.at[1]

    def settle(sem, ref):
        pltpu.make_async_copy(ref, ref, sem).wait()

    def remote(src, dst, ssem, rsem, device):
        copy = pltpu.make_async_remote_copy(
            src_ref=src, dst_ref=dst, send_sem=ssem, recv_sem=rsem,
            device_id=device, device_id_type=pl.DeviceIdType.MESH,
        )
        copy.start()
        return copy

    ins = (tok_in, cot_in)
    for tc in range(2):
        for j in range(STAGES):
            pltpu.make_async_copy(
                ins[tc].at[pl.ds(16 * j, 16)],
                panel.at[j, tc, zl // 2, y, zl % 2],
                load_sem.at[3],
            ).start()
    loads = []
    for i, (src, dst) in enumerate(((wg_in, wg), (wu_in, wu), (wd_in, wd))):
        loads.append(pltpu.make_async_copy(src, dst.at[0], load_sem.at[i]))
        loads[-1].start()

    barrier = pltpu.get_barrier_semaphore()
    peers = [at(dk=1), at(dz4=1)]
    peers += [at(dx=d) for d in (1, 2, 3)]
    peers += [at(dy=d) for d in (1, 2, 3)]
    peers += [at(dz=d) for d in (1, 2, 3)]
    for peer in peers:
        pl.semaphore_signal(barrier, inc=1, device_id=peer, device_id_type=pl.DeviceIdType.MESH)
    pl.semaphore_wait(barrier, len(peers))

    def tile(j, tc, t):
        ll = (zl - t + 4) % 4
        return panel.at[j, tc, ll // 2, y, ll % 2]

    def send_z(j, tc):
        for d in (1, 3, 2):
            remote(
                ins[tc].at[pl.ds(16 * j, 16)], tile(j, tc, 0),
                azs, azr0.at[tc, d - 1] if j == 0 else azr.at[j, tc], at(dz=d),
            )

    def send_y_tile(tc, t):
        src = tile(0, tc, t) if t else ins[tc].at[pl.ds(0, 16)]
        for d in (2, 1, 3):
            remote(src, tile(0, tc, t), ats, atr.at[tc], at(dy=d))

    wx = []

    def send_weights():
        for i, (src, dst) in enumerate(((wg_in, wg), (wu_in, wu), (wd_in, wd))):
            wx.append(remote(src, dst.at[1], wsend.at[i], wrecv.at[i], at(dk=1)))

    def own_tiles():
        settle(load_sem.at[3], rs_z.at[0])

    def gather_y(j, tc):
        if j == 0:
            for t in (1, 3, 2):
                settle(azr0.at[tc, t - 1], tile(j, tc, t))
                send_y_tile(tc, t)
            return
        settle(azr.at[j, tc], rs_z.at[j, tc])
        for d in (2, 1, 3):
            remote(
                panel.at[j, tc, :, y], panel.at[j, tc, :, y], ays, ayr.at[j, tc], at(dy=d),
            )

    def forward_core(j, tc):
        settle(atr.at[tc] if j == 0 else ayr.at[j, tc], rs_z.at[pl.ds(0, 2)])
        remote(panel.at[j, tc, 1 - k], other.at[j, tc], afs, afr.at[j, tc], at(dk=1))

    def partial(j, a):
        tc = 0 if a < 2 else 1
        if a != 1:
            settle(afr.at[j, tc], other.at[j, tc])
        if j == 0:
            loads[a].wait()
            wx[a].wait_recv()
        lhs0 = panel[j, tc, k].reshape(128, 384)
        lhs1 = other[j, tc].reshape(128, 384)
        w = (wg, wu, wd)[a]
        if a < 2:
            res = dot(lhs0, w[0], ((1,), (0,))) + dot(lhs1, w[1], ((1,), (0,)))
        else:
            res = dot(lhs0, w[0], ((1,), (1,))) + dot(lhs1, w[1], ((1,), (1,)))
        part_own[j, a] = res.reshape(4, 32, 896)
        part[j, a] = res.astype(BF16).reshape(4, 32, 896)
        for d in (2, 1, 3):
            remote(
                part.at[j, a, (x + d) % 4], rs_x.at[j, a, d - 1], xrs, xrr.at[j, a], at(dx=d),
            )

    def sum_x(j, a):
        settle(xrr.at[j, a], rs_x.at[j, a])
        total = part_own[j, a, x]
        for d in (1, 2, 3):
            total = total + rs_x[j, a, d - 1].astype(F32)
        part_own[j, a, x] = total
        zs[j, a] = total.astype(BF16)
        remote(zs.at[j, a], zr.at[j, a], z4s, z4r.at[j, a], at(dz4=1))

    def spread(j, a, value):
        hid[j, a, k, x] = value.astype(BF16)
        for d in (1, 3):
            remote(
                hid.at[j, a, k, x], hid.at[j, a, k, x], xas, xar.at[j, a, d // 2], at(dx=d),
            )

    def gate_up(j):
        return tuple(part_own[j, a, x] + zr[j, a].astype(F32) for a in range(2))

    def forward(j):
        settle(z4r.at[j, 0], zr.at[j, 0])
        settle(z4r.at[j, 1], zr.at[j, 1])
        gate, up = gate_up(j)
        spread(j, 0, gate * jax.nn.sigmoid(gate) * up)

    def backward(j):
        settle(z4r.at[j, 2], zr.at[j, 2])
        gate, up = gate_up(j)
        sig = jax.nn.sigmoid(gate)
        d_hidden = part_own[j, 2, x] + zr[j, 2].astype(F32)
        spread(j, 1, d_hidden * up * sig * (1.0 + gate * (1.0 - sig)))
        spread(j, 2, d_hidden * gate * sig)

    def relay(j, a):
        for d, half in ((1, 0), (3, 1)):
            settle(xar.at[j, a, half], hid.at[j, a, k, (x + 4 - d) % 4])
            piece = hid.at[j, a, k, (x + 4 - d) % 4, pl.ds(16 * half, 16)]
            remote(piece, piece, xas, xbr.at[j, a], at(dx=d))

    def forward_hidden(j, a):
        settle(xbr.at[j, a], hid.at[j, a, k, (x + 2) % 4])
        remote(hid.at[j, a, k], hid.at[j, a, k], hfs, hfr.at[j, a], at(dk=1))

    def stage_hidden(j, a):
        return hid[j, a].reshape(256, 896)

    def send_y(j, b, res):
        res = res.reshape(2, 4, 32, 384)
        oparts_own[j, b] = res
        oparts[j, b] = res.astype(BF16)
        for d in (2, 1, 3):
            remote(
                oparts.at[j, b, :, (y + d) % 4], rs_y.at[j, b, d - 1], yrs, yrr.at[j, b], at(dy=d),
            )

    def project(j, b):
        if b == 0:
            settle(hfr.at[j, 0], hid.at[j, 0, 1 - k])
            send_y(j, 0, dot(stage_hidden(j, 0), wd[0], ((1,), (0,))))
        else:
            settle(hfr.at[j, 1], hid.at[j, 1, 1 - k])
            settle(hfr.at[j, 2], hid.at[j, 2, 1 - k])
            send_y(j, 1, dot(stage_hidden(j, 1), wg[0], ((1,), (1,)))
                   + dot(stage_hidden(j, 2), wu[0], ((1,), (1,))))

    def grads(j, i):
        tok = panel[j, 0].reshape(256, 384)
        cot = panel[j, 1].reshape(256, 384)
        acc, l, r = (
            (gg, tok, stage_hidden(j, 1)),
            (gu, tok, stage_hidden(j, 2)),
            (gd, stage_hidden(j, 0), cot),
        )[i]
        term = dot(l, r, ((0,), (0,)))
        if j > 0:
            term = acc[...] + term
        if j == STAGES - 1:
            term = term * scale
        acc[...] = term

    def sum_y(j, b):
        settle(yrr.at[j, b], rs_y.at[j, b])
        total = oparts_own[j, b, :, y]
        for d in (1, 2, 3):
            total = total + rs_y[j, b, d - 1].astype(F32)
        oparts_own[j, b, :, y] = total
        zout[j, b] = total.astype(zout.dtype).reshape(4, 16, 384)
        for d in (2, 1, 3):
            remote(
                zout.at[j, b, (zl + d) % 4], rs_z.at[j, b, d - 1], zrs, zrr.at[j, b], at(dz=d),
            )

    def finish(j, b):
        settle(zrr.at[j, b], rs_z.at[j, b])
        total = oparts_own[j, b, zl // 2, y, pl.ds(pl.multiple_of(zl % 2 * 16, 16), 16)]
        for d in (1, 2, 3):
            total = total + rs_z[j, b, d - 1].astype(F32)
        (out_ref, gin_ref)[b][pl.ds(16 * j, 16)] = total.astype(BF16)

    def store(i):
        src = (out_ref, gin_ref, gg, gu, gd)[i]
        dst = (out_any, gin_any, gg_any, gu_any, gd_any)[i]
        pltpu.make_async_copy(src, dst, store_sem.at[(0, 0, 1, 1, 2)[i]]).start()

    steps = (
        (send_z, 0, 0), (send_y_tile, 0, 0), (send_z, 0, 1), (send_y_tile, 1, 0), (send_weights,),
        (send_z, 1, 0), (send_z, 1, 1), (send_z, 2, 0), (send_z, 2, 1),
        (gather_y, 0, 0), (gather_y, 0, 1), (own_tiles,), (gather_y, 1, 0), (forward_core, 0, 0), (gather_y, 1, 1),
        (partial, 0, 0), (partial, 0, 1), (forward_core, 0, 1), (gather_y, 2, 0), (gather_y, 2, 1),
        (forward_core, 1, 0), (partial, 0, 2), (forward_core, 1, 1), (partial, 1, 0), (partial, 1, 1), (partial, 1, 2),
        (sum_x, 0, 0), (sum_x, 0, 1), (forward_core, 2, 0), (forward_core, 2, 1), (partial, 2, 0), (partial, 2, 1), (partial, 2, 2),
        (sum_x, 0, 2), (sum_x, 1, 0), (forward, 0), (sum_x, 1, 1), (backward, 0), (sum_x, 1, 2), (sum_x, 2, 0), (forward, 1),
        (sum_x, 2, 1), (backward, 1), (sum_x, 2, 2),
        (relay, 0, 0), (relay, 0, 1), (forward, 2), (relay, 0, 2), (forward_hidden, 0, 0), (relay, 1, 0), (backward, 2),
        (forward_hidden, 0, 1), (relay, 1, 1), (forward_hidden, 0, 2), (relay, 1, 2), (forward_hidden, 1, 0),
        (project, 0, 0), (project, 0, 1), (grads, 0, 0), (relay, 2, 0), (forward_hidden, 1, 1), (forward_hidden, 1, 2),
        (grads, 0, 1), (grads, 0, 2), (project, 1, 0), (relay, 2, 1), (project, 1, 1), (relay, 2, 2), (sum_y, 0, 0), (sum_y, 0, 1),
        (forward_hidden, 2, 0), (project, 2, 0), (forward_hidden, 2, 1), (forward_hidden, 2, 2),
        (project, 2, 1), (sum_y, 1, 0), (sum_y, 1, 1), (grads, 1, 0), (grads, 1, 1), (grads, 1, 2), (finish, 0, 0), (finish, 0, 1),
        (sum_y, 2, 0), (grads, 2, 2), (store, 4), (grads, 2, 0), (store, 2), (grads, 2, 1), (store, 3), (sum_y, 2, 1),
        (finish, 1, 0), (finish, 1, 1), (finish, 2, 0), (store, 0), (finish, 2, 1), (store, 1),
    )
    for step, *where in steps:
        step(*where)
    settle(store_sem.at[0], rs_z.at[0])
    settle(store_sem.at[1], big)
    settle(store_sem.at[2], gd)
    for i, ref in enumerate((wg, wu, wd)):
        settle(wsend.at[i], ref.at[1])
    settle(azs, rs_z)
    settle(ats, zout)
    settle(ays, other)
    settle(afs, other)
    settle(xrs, rs_x)
    settle(z4s, zs)
    settle(xas, rs_x)
    settle(hfs, part)
    settle(yrs, rs_y)
    settle(zrs, rs_z)


def write_out(*refs):
    copies = [pltpu.make_async_copy(refs[i], refs[5 + i], refs[10].at[i]) for i in range(5)]
    for copy in copies:
        copy.start()
    for copy in copies:
        copy.wait()


def body(tokens, gate_weight, up_weight, down_weight, cotangent):
    total_tokens = tokens.shape[0] * lax.axis_size("col")
    scale = total_tokens ** (-0.5)
    vmem = pl.BlockSpec(memory_space=pltpu.VMEM)
    hbm = pl.BlockSpec(memory_space=pl.ANY)
    S = STAGES
    sem = pltpu.SemaphoreType.DMA
    scratch = [
        pltpu.VMEM((S, 2, 2, 4, 2, 16, 384), BF16),
        pltpu.VMEM((S, 2, 4, 2, 16, 384), BF16),
        pltpu.VMEM((2, 384, 896), BF16),
        pltpu.VMEM((2, 384, 896), BF16),
        pltpu.VMEM((2, 896, 384), BF16),
        pltpu.VMEM((S, 3, 4, 32, 896), BF16),
        pltpu.VMEM((S, 3, 4, 32, 896), F32),
        pltpu.VMEM((S, 3, 3, 32, 896), BF16),
        pltpu.VMEM((S, 3, 32, 896), BF16),
        pltpu.VMEM((S, 3, 32, 896), BF16),
        pltpu.VMEM((S, 3, 2, 4, 32, 896), BF16),
        pltpu.VMEM((S, 2, 2, 4, 32, 384), BF16),
        pltpu.VMEM((S, 2, 2, 4, 32, 384), F32),
        pltpu.VMEM((S, 2, 3, 2, 32, 384), BF16),
        pltpu.VMEM((S, 2, 4, 16, 384), BF16),
        pltpu.VMEM((S, 2, 3, 16, 384), BF16),
        pltpu.VMEM((48, 384), BF16),
        pltpu.VMEM((48, 384), BF16),
        pltpu.VMEM((2, 384, 896), F32),
        pltpu.VMEM((896, 384), F32),
        sem((4,)), sem((3,)), sem((3,)),
        sem(()), sem((S, 2)), sem((2, 3)), sem(()), sem((2,)), sem(()), sem((S, 2)), sem(()), sem((S, 2)),
        sem(()), sem((S, 3)), sem(()), sem((S, 3)), sem(()), sem((S, 3, 2)), sem((S, 3)), sem(()), sem((S, 3)),
        sem(()), sem((S, 2)), sem(()), sem((S, 2)), sem((3,)),
    ]
    results = pl.pallas_call(
        functools.partial(kernel, scale),
        out_shape=(
            pltpu.VMEM((48, 384), BF16),
            pltpu.VMEM((48, 384), BF16),
            pltpu.VMEM((384, 896), F32),
            pltpu.VMEM((384, 896), F32),
            pltpu.VMEM((896, 384), F32),
        ),
        in_specs=[pl.BlockSpec(memory_space=pltpu.HBM)] * 5,
        out_specs=(hbm,) * 5,
        scratch_shapes=scratch,
        compiler_params=pltpu.CompilerParams(
            collective_id=0, has_side_effects=True, vmem_limit_bytes=36 * 1024 * 1024,
        ),
        cost_estimate=pl.CostEstimate(
            flops=2 * 9 * 768 * 384 * 896, bytes_accessed=8 * 1024 * 1024, transcendentals=0,
        ),
        name="ffn",
    )(*(
        pltpu.with_memory_space_constraint(a, pltpu.HBM)
        for a in (tokens, gate_weight, up_weight, down_weight, cotangent)
    ))
    return pl.pallas_call(
        write_out,
        out_shape=tuple(jax.ShapeDtypeStruct(r.shape, r.dtype) for r in results),
        in_specs=[vmem] * 5,
        out_specs=(hbm,) * 5,
        scratch_shapes=[sem((5,))],
        compiler_params=pltpu.CompilerParams(vmem_limit_bytes=1024 * 1024),
        name="write_out",
    )(*results)


def solution(mesh):
    return jax.shard_map(
        body,
        mesh=mesh,
        in_specs=(
            P("col", "row"),
            P("row", "col"),
            P("row", "col"),
            P("col", "row"),
            P("col", "row"),
        ),
        out_specs=(
            P("col", "row"),
            P("col", "row"),
            P("row", "col"),
            P("row", "col"),
            P("col", "row"),
        ),
        check_vma=False,
    )
```

```python
import functools

import jax
import jax.numpy as jnp
from jax import lax
from jax.experimental import pallas as pl
from jax.experimental.pallas import tpu as pltpu
from jax.sharding import PartitionSpec as P

TILES = 3
STRAIGHT = (0,)
WHOLE = (3,)
BF16 = jnp.bfloat16
F32 = jnp.float32


def dot(a, b, dims):
    return lax.dot_general(a, b, (dims, ((), ())), preferred_element_type=F32)


STRIPS = (
    ((0, 0), (0, 1)),
    ((1, 0), (1, 1), (3, 0), (3, 1)),
    ((0, 2), (1, 2), (3, 2), (2, 0)),
    ((2, 1), (2, 2)),
)
STAGES = len(STRIPS)
SMALL = (0, 3)


def kernel(
    scale,
    tok_in, wg_in, wu_in, wd_in, cot_in,
    out_any, gin_any, gg_any, gu_any, gd_any,
    panel, other, wg, wu, wd,
    part_s, part_l, own_s, own_l, pairs_s, pairs_l, rs_x_s, rs_x_l, zs_s, zs_l, zr_s, zr_l, hid_s, hid_l,
    oparts, oparts_own, rs_y, zout, zout_b, rs_z, rs_z_b,
    out_ref, gin_ref, big, gd,
    load_sem, wsend, wrecv,
    azs, azr, azr_b, ats, atr, ays, ayr, ayr_b, afs, afr,
    xrs, xpr, xrr, z4s, z4r, xas, xar, xbr, hfs, hfr,
    yrs, yrr, zrs, zrr, store_sem,
):
    row = lax.axis_index("row")
    col = lax.axis_index("col")
    x = row // 4
    zh = (row // 2) % 2
    k = row % 2
    y = col // 4
    zl = col % 4
    turn = 1 + 2 * k

    def at(dx=0, dz4=0, dk=0, dy=0, dz=0):
        xx = (x + dx) % 4
        zz = (zh + dz4) % 2
        kk = (k + dk) % 2
        yy = (y + dy) % 4
        ll = (zl + dz) % 4
        return {"row": xx * 4 + zz * 2 + kk, "col": yy * 4 + ll}

    def pick(s, small, large):
        return small.at[SMALL.index(s)] if s in SMALL else large.at[s - 1]

    def kind(s):
        return 0 if s in SMALL else 1

    part = [pick(s, part_s, part_l) for s in range(STAGES)]
    part_own = [pick(s, own_s, own_l) for s in range(STAGES)]
    pairs = [pick(s, pairs_s, pairs_l) for s in range(STAGES)]
    rs_x = [pick(s, rs_x_s, rs_x_l) for s in range(STAGES)]
    zs = [pick(s, zs_s, zs_l) for s in range(STAGES)]
    zr = [pick(s, zr_s, zr_l) for s in range(STAGES)]
    hid = [pick(s, hid_s, hid_l) for s in range(STAGES)]
    gg, gu = big.at[0], big.at[1]

    def settle(sem, ref):
        pltpu.make_async_copy(ref, ref, sem).wait()

    def remote(src, dst, ssem, rsem, device):
        copy = pltpu.make_async_remote_copy(
            src_ref=src, dst_ref=dst, send_sem=ssem, recv_sem=rsem,
            device_id=device, device_id_type=pl.DeviceIdType.MESH,
        )
        copy.start()
        return copy

    ins = (tok_in, cot_in)
    first, last = pl.ds(0, 2), pl.ds(2, 1)
    for tc in range(2):
        pltpu.make_async_copy(ins[tc], panel.at[:, tc, zl // 2, y, zl % 2], load_sem.at[3]).start()
    loads = []
    for i, (src, dst) in enumerate(((wg_in, wg), (wu_in, wu), (wd_in, wd))):
        loads.append(pltpu.make_async_copy(src, dst.at[0], load_sem.at[i]))
        loads[-1].start()

    barrier = pltpu.get_barrier_semaphore()
    peers = [at(dk=1), at(dz4=1)]
    peers += [at(dx=d) for d in (1, 2, 3)]
    peers += [at(dy=d) for d in (1, 2, 3)]
    peers += [at(dz=d) for d in (1, 2, 3)]
    for peer in peers:
        pl.semaphore_signal(barrier, inc=1, device_id=peer, device_id_type=pl.DeviceIdType.MESH)
    pl.semaphore_wait(barrier, len(peers))

    def tiles(js, tc, t):
        ll = (zl - t + 4) % 4
        return panel.at[js, tc, ll // 2, y, ll % 2]

    def send_z(late, tc):
        js = last if late else first
        for d in (1, 3, 2):
            remote(
                ins[tc].at[js], tiles(js, tc, 0),
                azs, azr_b.at[tc] if late else azr.at[tc, d - 1], at(dz=d),
            )

    def send_near(tc, t):
        src = tiles(first, tc, t) if t else ins[tc].at[first]
        for d in (1, 3):
            remote(src, tiles(first, tc, t), ats, atr.at[tc], at(dy=d))

    wx = []

    def send_weights():
        for i, (src, dst) in enumerate(((wg_in, wg), (wu_in, wu), (wd_in, wd))):
            wx.append(remote(src, dst.at[1], wsend.at[i], wrecv.at[i], at(dk=1)))

    def own_tiles():
        settle(load_sem.at[3], other.at[:, :, 0, 0])

    def gather_near(tc):
        for t in (1, 3, 2):
            settle(azr.at[tc, t - 1], tiles(first, tc, t))
            send_near(tc, t)

    def gather_last(tc):
        settle(azr_b.at[tc], other.at[0, tc, pl.ds(0, 3), 0])
        block = panel.at[last, tc, :, y]
        for d in (1, 3):
            remote(block, block, ays.at[0], ayr_b.at[tc, 0], at(dy=d))

    def gather_far(tc):
        block = panel.at[pl.ds(0, 1), tc, :, y]
        remote(block, block, ays.at[0], ayr.at[tc], at(dy=2))

    def gather_end(tc):
        block = panel.at[pl.ds(1, 2), tc, :, y]
        remote(block, block, ays.at[1], ayr_b.at[tc, 1], at(dy=2))

    def forward_core(s, tc):
        if s == 1:
            settle(atr.at[tc], other.at[0])
        if s == 2:
            settle(ayr_b.at[tc, 0], other.at[0, tc])
            settle(ayr.at[tc], other.at[0, tc, pl.ds(0, 2)])
        if s == 3:
            settle(ayr_b.at[tc, 1], other.at[0, tc])
        for dy in sorted({dy for dy, _ in STRIPS[s]}):
            js = [j for d, j in STRIPS[s] if d == dy]
            js = pl.ds(js[0], len(js))
            yy = (y + dy) % 4
            remote(panel.at[js, tc, 1 - k, yy], other.at[js, tc, yy], afs, afr.at[s, tc], at(dk=1))

    def partial(s, a):
        tc = 0 if a < 2 else 1
        n = len(STRIPS[s])
        if a != 1:
            settle(afr.at[s, tc], other.at[0, tc, pl.ds(0, n)])
        if s == 0:
            loads[a].wait()
            wx[a].wait_recv()
        lhs0 = jnp.concatenate([panel[j, tc, k, (y + dy) % 4].reshape(32, 384) for dy, j in STRIPS[s]])
        lhs1 = jnp.concatenate([other[j, tc, (y + dy) % 4].reshape(32, 384) for dy, j in STRIPS[s]])
        w = (wg, wu, wd)[a]
        if a < 2:
            res = dot(lhs0, w[0], ((1,), (0,))) + dot(lhs1, w[1], ((1,), (0,)))
        else:
            res = dot(lhs0, w[0], ((1,), (1,))) + dot(lhs1, w[1], ((1,), (1,)))
        part_own[s][a] = res.reshape(4, 8 * n, 896)
        part[s][a] = res.astype(BF16).reshape(4, 8 * n, 896)
        ssem = xrs.at[kind(s)]
        if s in STRAIGHT:
            if s in SMALL:
                remote(part[s].at[a, (x + 2) % 4], pairs[s].at[a, 0], ssem, xpr.at[s, a, 0], at(dx=2))
            else:
                for i in range(2):
                    remote(part[s].at[a, (x + 2) % 4, pl.ds(16 * i, 16)], pairs[s].at[a, i],
                           ssem, xpr.at[s, a, i], at(dx=2))
            for i, d in enumerate((1, 3)):
                remote(part[s].at[a, (x + d) % 4], rs_x[s].at[a, i], ssem, xrr.at[s, a], at(dx=d))
        elif s in SMALL:
            remote(part[s].at[a, (x + 2) % 4], pairs[s].at[a, 0], ssem, xpr.at[s, a, 0], at(dx=turn))
            remote(part[s].at[a, (x + 4 - turn) % 4], rs_x[s].at[a, 1], ssem, xrr.at[s, a], at(dx=4 - turn))
        else:
            for i, d in enumerate((1, 3)):
                remote(part[s].at[a, (x + 2) % 4, pl.ds(16 * i, 16)], pairs[s].at[a, i],
                       ssem, xpr.at[s, a, i], at(dx=d))
            for i, d in enumerate((1, 3)):
                rows = pl.ds(16 - 16 * i, 16)
                remote(part[s].at[a, (x + d) % 4, rows], rs_x[s].at[a, i, rows], ssem, xrr.at[s, a], at(dx=d))

    def pass_on(s, a):
        ssem = xrs.at[kind(s)]
        if s in SMALL:
            settle(xpr.at[s, a, 0], pairs[s].at[a, 0])
            both = part_own[s][a, (x + turn) % 4] + pairs[s][a, 0].astype(F32)
            part[s][a, (x + turn) % 4] = both.astype(BF16)
            remote(part[s].at[a, (x + turn) % 4], rs_x[s].at[a, 0], ssem, xrr.at[s, a], at(dx=turn))
            return
        for i, d in enumerate((1, 3)):
            settle(xpr.at[s, a, i], pairs[s].at[a, i])
            rows = pl.ds(16 * i, 16)
            both = part_own[s][a, (x + d) % 4, rows] + pairs[s][a, i].astype(F32)
            part[s][a, (x + d) % 4, rows] = both.astype(BF16)
            remote(part[s].at[a, (x + d) % 4, rows], rs_x[s].at[a, i, rows], ssem, xrr.at[s, a], at(dx=d))

    def sum_x(s, a):
        settle(xrr.at[s, a], rs_x[s].at[a])
        total = part_own[s][a, x] + rs_x[s][a, 0].astype(F32) + rs_x[s][a, 1].astype(F32)
        if s in STRAIGHT:
            for i in range(1 if s in SMALL else 2):
                settle(xpr.at[s, a, i], pairs[s].at[a, i])
            total = total + pairs[s][a].reshape(total.shape).astype(F32)
        part_own[s][a, x] = total
        zs[s][a] = total.astype(BF16)
        remote(zs[s].at[a], zr[s].at[a], z4s.at[kind(s)], z4r.at[s, a], at(dz4=1))

    def spread(s, a, value):
        hid[s][a, k, x] = value.astype(BF16)
        piece = hid[s].at[a, k, x]
        if s in WHOLE:
            remote(piece, piece, xas.at[kind(s)], xbr.at[s, a], at(dx=2))
        for d in (1, 3):
            remote(piece, piece, xas.at[kind(s)], xar.at[s, a, d // 2], at(dx=d))

    def gate_up(s):
        return tuple(part_own[s][a, x] + zr[s][a].astype(F32) for a in range(2))

    def forward(s):
        settle(z4r.at[s, 0], zr[s].at[0])
        settle(z4r.at[s, 1], zr[s].at[1])
        gate, up = gate_up(s)
        spread(s, 0, gate * jax.nn.sigmoid(gate) * up)

    def backward(s):
        settle(z4r.at[s, 2], zr[s].at[2])
        gate, up = gate_up(s)
        sig = jax.nn.sigmoid(gate)
        d_hidden = part_own[s][2, x] + zr[s][2].astype(F32)
        spread(s, 1, d_hidden * up * sig * (1.0 + gate * (1.0 - sig)))
        spread(s, 2, d_hidden * gate * sig)

    def relay(s, a):
        if s in SMALL:
            for i, d in enumerate((1, 3)):
                settle(xar.at[s, a, i], hid[s].at[a, k, (x + 4 - d) % 4])
            piece = hid[s].at[a, k, (x + 4 - turn) % 4]
            remote(piece, piece, xas.at[0], xbr.at[s, a], at(dx=turn))
            return
        for i, d in enumerate((1, 3)):
            settle(xar.at[s, a, i], hid[s].at[a, k, (x + 4 - d) % 4])
            piece = hid[s].at[a, k, (x + 4 - d) % 4, pl.ds(16 * i, 16)]
            remote(piece, piece, xas.at[1], xbr.at[s, a], at(dx=d))

    def forward_hidden(s, a):
        if s in WHOLE:
            for i, d in enumerate((1, 3)):
                settle(xar.at[s, a, i], hid[s].at[a, k, (x + 4 - d) % 4])
        settle(xbr.at[s, a], hid[s].at[a, k, (x + 2) % 4])
        remote(hid[s].at[a, k], hid[s].at[a, k], hfs.at[kind(s)], hfr.at[s, a], at(dk=1))

    def take(s, a):
        settle(hfr.at[s, a], hid[s].at[a, 1 - k])

    def project(s, b, other_core):
        n = len(STRIPS[s])
        kk = 1 - k if other_core else k
        if b == 0:
            res = dot(hid[s][0, kk].reshape(32 * n, 896), wd[0], ((1,), (0,)))
        else:
            res = (dot(hid[s][1, kk].reshape(32 * n, 896), wg[0], ((1,), (1,)))
                   + dot(hid[s][2, kk].reshape(32 * n, 896), wu[0], ((1,), (1,))))
        res = res.reshape(n, 32, 384)
        for i, (dy, j) in enumerate(STRIPS[s]):
            oparts_own[j, b, kk, (y + dy) % 4] = res[i]
            if dy:
                oparts[j, b, kk, (y + dy) % 4] = res[i].astype(BF16)
                remote(
                    oparts.at[j, b, kk, (y + dy) % 4], rs_y.at[j, b, dy - 1, kk],
                    yrs, yrr.at[j, b], at(dy=dy),
                )

    def grads(s, i):
        n = len(STRIPS[s])

        def rows(tc):
            return jnp.concatenate(
                [panel[j, tc, kk, (y + dy) % 4].reshape(32, 384) for kk in range(2) for dy, j in STRIPS[s]]
            )

        def units(a):
            return hid[s][a].reshape(64 * n, 896)

        if i < 2:
            acc, term = (gg, gu)[i], dot(rows(0), units(1 + i), ((0,), (0,)))
        else:
            acc, term = gd, dot(units(0), rows(1), ((0,), (0,)))
        if s > 0:
            term = acc[...] + term
        if s == STAGES - 1:
            term = term * scale
        acc[...] = term

    def sums(j):
        return (zout_b, rs_z_b, j - 1, zrs.at[1]) if j else (zout, rs_z, 0, zrs.at[0])

    def sum_y(j, b):
        settle(yrr.at[j, b], rs_y.at[j, b])
        total = oparts_own[j, b, :, y]
        for d in (1, 2, 3):
            total = total + rs_y[j, b, d - 1].astype(F32)
        oparts_own[j, b, :, y] = total
        mine, theirs, i, ssem = sums(j)
        mine[i, b] = total.astype(mine.dtype).reshape(4, 16, 384)
        for d in (2, 1, 3):
            remote(mine.at[i, b, (zl + d) % 4], theirs.at[i, b, d - 1], ssem, zrr.at[j, b], at(dz=d))

    def finish(j, b):
        mine, theirs, i, ssem = sums(j)
        settle(zrr.at[j, b], theirs.at[i, b])
        total = oparts_own[j, b, zl // 2, y, pl.ds(pl.multiple_of(zl % 2 * 16, 16), 16)]
        for d in (1, 2, 3):
            total = total + theirs[i, b, d - 1].astype(F32)
        (out_ref, gin_ref)[b][pl.ds(16 * j, 16)] = total.astype(BF16)

    def store(i):
        src = (out_ref, gin_ref, gg, gu, gd)[i]
        dst = (out_any, gin_any, gg_any, gu_any, gd_any)[i]
        pltpu.make_async_copy(src, dst, store_sem.at[(0, 0, 1, 1, 2)[i]]).start()

    steps = (
        (send_z, 0, 0), (send_near, 1, 0), (send_z, 1, 0), (own_tiles,), (send_near, 0, 0), (send_weights,),
        (send_z, 0, 1), (gather_near, 0), (forward_core, 0, 0), (gather_last, 0), (send_z, 1, 1), (partial, 0, 0),
        (gather_near, 1), (forward_core, 0, 1), (partial, 0, 1), (forward_core, 1, 0), (gather_far, 0),
        (gather_end, 0), (partial, 0, 2), (partial, 1, 0), (partial, 1, 1), (sum_x, 0, 0), (forward_core, 1, 1),
        (sum_x, 0, 1), (sum_x, 0, 2), (gather_far, 1), (forward_core, 2, 0), (gather_last, 1), (pass_on, 1, 0),
        (gather_end, 1), (partial, 1, 2), (forward_core, 3, 0), (pass_on, 1, 1), (partial, 2, 0), (partial, 2, 1),
        (sum_x, 1, 0), (pass_on, 1, 2), (forward_core, 2, 1), (sum_x, 1, 1), (forward, 0), (partial, 3, 0),
        (pass_on, 2, 0), (pass_on, 2, 1), (partial, 2, 2), (sum_x, 1, 2), (partial, 3, 1), (backward, 0),
        (forward_core, 3, 1), (sum_x, 2, 0), (pass_on, 2, 2), (sum_x, 2, 1), (relay, 0, 0), (partial, 3, 2),
        (pass_on, 3, 0), (pass_on, 3, 1), (forward, 1), (relay, 0, 2), (relay, 0, 1), (sum_x, 2, 2), (pass_on, 3, 2),
        (backward, 1), (sum_x, 3, 0), (relay, 1, 0), (forward_hidden, 0, 0), (forward_hidden, 0, 1),
        (forward_hidden, 0, 2), (sum_x, 3, 1), (project, 0, 1, 0), (sum_x, 3, 2), (relay, 1, 1), (relay, 1, 2),
        (forward, 2), (forward_hidden, 1, 0), (backward, 2), (take, 0, 1), (forward_hidden, 1, 1), (take, 1, 0),
        (take, 0, 2), (forward_hidden, 1, 2), (project, 1, 1, 0), (project, 1, 0, 1), (relay, 2, 0), (forward, 3),
        (project, 1, 0, 0), (backward, 3), (grads, 0, 0), (take, 1, 1), (take, 1, 2), (project, 1, 1, 1),
        (relay, 2, 1), (relay, 2, 2), (forward_hidden, 2, 0), (project, 2, 0, 0), (forward_hidden, 3, 0),
        (project, 3, 0, 0), (take, 0, 0), (project, 0, 1, 1), (take, 2, 0), (project, 2, 0, 1), (project, 0, 0, 1),
        (grads, 0, 2), (take, 3, 0), (project, 3, 0, 1), (forward_hidden, 3, 1), (forward_hidden, 3, 2),
        (project, 3, 1, 0), (forward_hidden, 2, 1), (forward_hidden, 2, 2), (project, 2, 1, 0), (project, 0, 0, 0),
        (take, 3, 2), (take, 3, 1), (project, 3, 1, 1), (take, 2, 1), (grads, 1, 2), (take, 2, 2), (sum_y, 0, 0),
        (project, 2, 1, 1), (grads, 0, 1), (grads, 1, 1), (grads, 2, 1), (sum_y, 1, 0), (sum_y, 2, 0), (grads, 3, 1),
        (grads, 2, 2), (sum_y, 1, 1), (sum_y, 2, 1), (store, 3), (grads, 3, 2), (sum_y, 0, 1), (grads, 1, 0),
        (finish, 2, 0), (finish, 2, 1), (grads, 2, 0), (finish, 1, 1), (grads, 3, 0), (finish, 1, 0), (finish, 0, 0),
        (store, 2), (store, 4), (store, 0), (finish, 0, 1), (store, 1),
    )
    for step, *where in steps:
        step(*where)
    settle(store_sem.at[0], other.at[:, :, 0, 0])
    settle(store_sem.at[1], big)
    settle(store_sem.at[2], gd)
    for i, ref in enumerate((wg, wu, wd)):
        settle(wsend.at[i], ref.at[1])
    settle(azs, other.at[:, :, pl.ds(0, 3), 0])
    settle(ats, other.at[pl.ds(0, 2)])
    settle(ays.at[0], other.at[:, :, :, 0])
    settle(ays.at[1], other.at[0])
    settle(afs, other)
    for i, ref in enumerate((part_s, part_l)):
        settle(xrs.at[i], ref.at[:, :, pl.ds(0, 3)])
        settle(xas.at[i], ref.at[:, :, pl.ds(0, 3)])
        settle(hfs.at[i], ref)
        settle(z4s.at[i], (zs_s, zs_l)[i])
        settle(zrs.at[i], (rs_z, rs_z_b)[i])
    settle(yrs, rs_y)


def write_out(*refs):
    copies = [pltpu.make_async_copy(refs[i], refs[5 + i], refs[10].at[i]) for i in range(5)]
    for copy in copies:
        copy.start()
    for copy in copies:
        copy.wait()


def body(tokens, gate_weight, up_weight, down_weight, cotangent):
    total_tokens = tokens.shape[0] * lax.axis_size("col")
    scale = total_tokens ** (-0.5)
    vmem = pl.BlockSpec(memory_space=pltpu.VMEM)
    hbm = pl.BlockSpec(memory_space=pl.ANY)
    sem = pltpu.SemaphoreType.DMA
    both = lambda *shape, dtype=BF16: [pltpu.VMEM((2, 3, *shape, r, 896), dtype) for r in (16, 32)]
    scratch = [
        pltpu.VMEM((TILES, 2, 2, 4, 2, 16, 384), BF16),
        pltpu.VMEM((TILES, 2, 4, 2, 16, 384), BF16),
        pltpu.VMEM((2, 384, 896), BF16),
        pltpu.VMEM((2, 384, 896), BF16),
        pltpu.VMEM((2, 896, 384), BF16),
        *both(4), *both(4, dtype=F32),
        pltpu.VMEM((2, 3, 1, 16, 896), BF16),
        pltpu.VMEM((2, 3, 2, 16, 896), BF16),
        *both(2), *both(), *both(), *both(2, 4),
        pltpu.VMEM((TILES, 2, 2, 4, 32, 384), BF16),
        pltpu.VMEM((TILES, 2, 2, 4, 32, 384), F32),
        pltpu.VMEM((TILES, 2, 3, 2, 32, 384), BF16),
        pltpu.VMEM((1, 2, 4, 16, 384), F32),
        pltpu.VMEM((2, 2, 4, 16, 384), BF16),
        pltpu.VMEM((1, 2, 3, 16, 384), F32),
        pltpu.VMEM((2, 2, 3, 16, 384), BF16),
        pltpu.VMEM((48, 384), BF16),
        pltpu.VMEM((48, 384), BF16),
        pltpu.VMEM((2, 384, 896), F32),
        pltpu.VMEM((896, 384), F32),
        sem((4,)), sem((3,)), sem((3,)),
        sem(()), sem((2, 3)), sem((2,)), sem(()), sem((2,)), sem((2,)), sem((2,)), sem((2, 2)), sem(()), sem((STAGES, 2)),
        sem((2,)), sem((STAGES, 3, 2)), sem((STAGES, 3)), sem((2,)), sem((STAGES, 3)),
        sem((2,)), sem((STAGES, 3, 2)), sem((STAGES, 3)), sem((2,)), sem((STAGES, 3)),
        sem(()), sem((TILES, 2)), sem((2,)), sem((TILES, 2)), sem((3,)),
    ]
    results = pl.pallas_call(
        functools.partial(kernel, scale),
        out_shape=(
            pltpu.VMEM((48, 384), BF16),
            pltpu.VMEM((48, 384), BF16),
            pltpu.VMEM((384, 896), F32),
            pltpu.VMEM((384, 896), F32),
            pltpu.VMEM((896, 384), F32),
        ),
        in_specs=[pl.BlockSpec(memory_space=pltpu.HBM)] * 5,
        out_specs=(hbm,) * 5,
        scratch_shapes=scratch,
        compiler_params=pltpu.CompilerParams(
            collective_id=0, has_side_effects=True, vmem_limit_bytes=36 * 1024 * 1024,
        ),
        cost_estimate=pl.CostEstimate(
            flops=2 * 9 * 768 * 384 * 896, bytes_accessed=8 * 1024 * 1024, transcendentals=0,
        ),
        name="ffn",
    )(*(
        pltpu.with_memory_space_constraint(a, pltpu.HBM)
        for a in (tokens.reshape(TILES, 16, 384), gate_weight, up_weight, down_weight,
                  cotangent.reshape(TILES, 16, 384))
    ))
    return pl.pallas_call(
        write_out,
        out_shape=tuple(jax.ShapeDtypeStruct(r.shape, r.dtype) for r in results),
        in_specs=[vmem] * 5,
        out_specs=(hbm,) * 5,
        scratch_shapes=[sem((5,))],
        compiler_params=pltpu.CompilerParams(vmem_limit_bytes=1024 * 1024),
        name="write_out",
    )(*results)


def solution(mesh):
    return jax.shard_map(
        body,
        mesh=mesh,
        in_specs=(
            P("col", "row"),
            P("row", "col"),
            P("row", "col"),
            P("col", "row"),
            P("col", "row"),
        ),
        out_specs=(
            P("col", "row"),
            P("col", "row"),
            P("row", "col"),
            P("row", "col"),
            P("col", "row"),
        ),
        check_vma=False,
    )
```

```python
import functools

import jax
import jax.numpy as jnp
from jax import lax
from jax.experimental import pallas as pl
from jax.experimental.pallas import tpu as pltpu
from jax.sharding import PartitionSpec as P

TILES = 3
STRAIGHT = (0,)
WHOLE = (0, 3)
BF16 = jnp.bfloat16
F32 = jnp.float32


def dot(a, b, dims):
    return lax.dot_general(a, b, (dims, ((), ())), preferred_element_type=F32)


STRIPS = (
    ((0, 0), (0, 1)),
    ((1, 0), (3, 0), (2, 0), (0, 2)),
    ((1, 1), (3, 1), (2, 1), (2, 2)),
    ((1, 2), (3, 2)),
)
STAGES = len(STRIPS)
SMALL = (0, 3)


def kernel(
    scale,
    tok_in, wg_in, wu_in, wd_in, cot_in,
    out_ref, gin_ref, gg, gu, gd,
    panel, other, wg, wu, wd,
    part_s, part_l, own_s, own_l, pairs_s, pairs_l, rs_x_s, rs_x_l, zs_s, zs_l, zr_s, zr_l, hid_s, hid_l,
    oparts, oparts_own, rs_y, zout, zout_b, rs_z, rs_z_b,
    load_sem, wsend, wrecv,
    azs, azr, azr_b, ats, atr, ays, ayr, ayr_b, afs, afr,
    xrs, xpr, xrr, z4s, z4r, xas, xar, xbr, hfs, hfr,
    yrs, yrr, zrs, zrr,
):
    row = lax.axis_index("row")
    col = lax.axis_index("col")
    x = row // 4
    zh = (row // 2) % 2
    k = row % 2
    y = col // 4
    zl = col % 4
    turn = 1 + 2 * k

    def at(dx=0, dz4=0, dk=0, dy=0, dz=0):
        xx = (x + dx) % 4
        zz = (zh + dz4) % 2
        kk = (k + dk) % 2
        yy = (y + dy) % 4
        ll = (zl + dz) % 4
        return {"row": xx * 4 + zz * 2 + kk, "col": yy * 4 + ll}

    def pick(s, small, large):
        return small.at[SMALL.index(s)] if s in SMALL else large.at[s - 1]

    def kind(s):
        return 0 if s in SMALL else 1

    part = [pick(s, part_s, part_l) for s in range(STAGES)]
    part_own = [pick(s, own_s, own_l) for s in range(STAGES)]
    pairs = [pick(s, pairs_s, pairs_l) for s in range(STAGES)]
    rs_x = [pick(s, rs_x_s, rs_x_l) for s in range(STAGES)]
    zs = [pick(s, zs_s, zs_l) for s in range(STAGES)]
    zr = [pick(s, zr_s, zr_l) for s in range(STAGES)]
    hid = [pick(s, hid_s, hid_l) for s in range(STAGES)]

    def settle(sem, ref):
        pltpu.make_async_copy(ref, ref, sem).wait()

    def remote(src, dst, ssem, rsem, device):
        copy = pltpu.make_async_remote_copy(
            src_ref=src, dst_ref=dst, send_sem=ssem, recv_sem=rsem,
            device_id=device, device_id_type=pl.DeviceIdType.MESH,
        )
        copy.start()
        return copy

    ins = (tok_in, cot_in)
    first, last = pl.ds(0, 2), pl.ds(2, 1)
    for tc in range(2):
        pltpu.make_async_copy(ins[tc], panel.at[:, tc, zl // 2, y, zl % 2], load_sem.at[3]).start()
    loads = []
    for i, (src, dst) in enumerate(((wg_in, wg), (wu_in, wu), (wd_in, wd))):
        loads.append(pltpu.make_async_copy(src, dst.at[0], load_sem.at[i]))
        loads[-1].start()

    barrier = pltpu.get_barrier_semaphore()
    peers = [at(dk=1), at(dz4=1)]
    peers += [at(dx=d) for d in (1, 2, 3)]
    peers += [at(dy=d) for d in (1, 2, 3)]
    peers += [at(dz=d) for d in (1, 2, 3)]
    for peer in peers:
        pl.semaphore_signal(barrier, inc=1, device_id=peer, device_id_type=pl.DeviceIdType.MESH)
    pl.semaphore_wait(barrier, len(peers))

    def tiles(js, tc, t):
        ll = (zl - t + 4) % 4
        return panel.at[js, tc, ll // 2, y, ll % 2]

    def send_z(late, tc):
        js = last if late else first
        for d in (1, 3, 2):
            remote(
                ins[tc].at[js], tiles(js, tc, 0),
                azs, azr_b.at[tc] if late else azr.at[tc, d - 1], at(dz=d),
            )

    def send_near(tc, t):
        src = tiles(0, tc, t) if t else ins[tc].at[0]
        for d in (1, 3, 2):
            remote(src, tiles(0, tc, t), ats, atr.at[tc], at(dy=d))

    wx = []

    def send_weights():
        for i, (src, dst) in enumerate(((wg_in, wg), (wu_in, wu), (wd_in, wd))):
            wx.append(remote(src, dst.at[1], wsend.at[i], wrecv.at[i], at(dk=1)))

    def own_tiles():
        settle(load_sem.at[3], other.at[:, :, 0, 0])

    def gather_near(tc):
        for t in (1, 3, 2):
            settle(azr.at[tc, t - 1], tiles(first, tc, t))
            send_near(tc, t)

    def take_last(tc):
        settle(azr_b.at[tc], other.at[0, tc, pl.ds(0, 3), 0])

    def gather_mid(tc):
        for d, js in ((1, pl.ds(1, 1)), (3, pl.ds(1, 1)), (2, pl.ds(1, 2))):
            block = panel.at[js, tc, :, y]
            remote(block, block, ays.at[0], ayr.at[tc], at(dy=d))

    def gather_end(tc):
        block = panel.at[last, tc, :, y]
        for d in (1, 3):
            remote(block, block, ays.at[1], ayr_b.at[tc], at(dy=d))

    def forward_core(s, tc):
        if s == 1:
            settle(atr.at[tc], other.at[:, :, pl.ds(0, 2), 0])
        if s == 2:
            settle(ayr.at[tc], other.at[0])
        if s == 3:
            settle(ayr_b.at[tc], other.at[0, tc])
        for dy in sorted({dy for dy, _ in STRIPS[s]}):
            js = [j for d, j in STRIPS[s] if d == dy]
            js = pl.ds(js[0], len(js))
            yy = (y + dy) % 4
            remote(panel.at[js, tc, 1 - k, yy], other.at[js, tc, yy], afs, afr.at[s, tc], at(dk=1))

    def partial(s, a):
        tc = 0 if a < 2 else 1
        n = len(STRIPS[s])
        if a != 1:
            settle(afr.at[s, tc], other.at[0, tc, pl.ds(0, n)])
        if s == 0:
            loads[a].wait()
            wx[a].wait_recv()
        lhs0 = jnp.concatenate([panel[j, tc, k, (y + dy) % 4].reshape(32, 384) for dy, j in STRIPS[s]])
        lhs1 = jnp.concatenate([other[j, tc, (y + dy) % 4].reshape(32, 384) for dy, j in STRIPS[s]])
        w = (wg, wu, wd)[a]
        if a < 2:
            res = dot(lhs0, w[0], ((1,), (0,))) + dot(lhs1, w[1], ((1,), (0,)))
        else:
            res = dot(lhs0, w[0], ((1,), (1,))) + dot(lhs1, w[1], ((1,), (1,)))
        part_own[s][a] = res.reshape(4, 8 * n, 896)
        part[s][a] = res.astype(BF16).reshape(4, 8 * n, 896)
        ssem = xrs.at[kind(s)]
        if s in STRAIGHT:
            if s in SMALL:
                remote(part[s].at[a, (x + 2) % 4], pairs[s].at[a, 0], ssem, xpr.at[s, a], at(dx=2))
            else:
                for i in range(2):
                    remote(part[s].at[a, (x + 2) % 4, pl.ds(16 * i, 16)], pairs[s].at[a, i],
                           ssem, xpr.at[s, a], at(dx=2))
            for i, d in enumerate((1, 3)):
                remote(part[s].at[a, (x + d) % 4], rs_x[s].at[a, i], ssem, xrr.at[s, a], at(dx=d))
        elif s in SMALL:
            remote(part[s].at[a, (x + 2) % 4], pairs[s].at[a, 0], ssem, xpr.at[s, a], at(dx=turn))
            remote(part[s].at[a, (x + 4 - turn) % 4], rs_x[s].at[a, 1], ssem, xrr.at[s, a], at(dx=4 - turn))
        else:
            for i, d in enumerate((1, 3)):
                remote(part[s].at[a, (x + 2) % 4, pl.ds(16 * i, 16)], pairs[s].at[a, i],
                       ssem, xpr.at[s, a], at(dx=d))
            for i, d in enumerate((1, 3)):
                rows = pl.ds(16 - 16 * i, 16)
                remote(part[s].at[a, (x + d) % 4, rows], rs_x[s].at[a, i, rows], ssem, xrr.at[s, a], at(dx=d))

    def pass_on(s, a):
        ssem = xrs.at[kind(s)]
        settle(xpr.at[s, a], pairs[s].at[a])
        if s in SMALL:
            both = part_own[s][a, (x + turn) % 4] + pairs[s][a, 0].astype(F32)
            part[s][a, (x + turn) % 4] = both.astype(BF16)
            remote(part[s].at[a, (x + turn) % 4], rs_x[s].at[a, 0], ssem, xrr.at[s, a], at(dx=turn))
            return
        for i, d in enumerate((1, 3)):
            rows = pl.ds(16 * i, 16)
            both = part_own[s][a, (x + d) % 4, rows] + pairs[s][a, i].astype(F32)
            part[s][a, (x + d) % 4, rows] = both.astype(BF16)
            remote(part[s].at[a, (x + d) % 4, rows], rs_x[s].at[a, i, rows], ssem, xrr.at[s, a], at(dx=d))

    def sum_x(s, a):
        settle(xrr.at[s, a], rs_x[s].at[a])
        total = part_own[s][a, x] + rs_x[s][a, 0].astype(F32) + rs_x[s][a, 1].astype(F32)
        if s in STRAIGHT:
            settle(xpr.at[s, a], pairs[s].at[a])
            total = total + pairs[s][a].reshape(total.shape).astype(F32)
        part_own[s][a, x] = total
        zs[s][a] = total.astype(BF16)
        remote(zs[s].at[a], zr[s].at[a], z4s.at[kind(s)], z4r.at[s, a // 2], at(dz4=1))

    def spread(s, a, value):
        hid[s][a, k, x] = value.astype(BF16)
        piece = hid[s].at[a, k, x]
        if s in WHOLE:
            remote(piece, piece, xas.at[kind(s)], xbr.at[s, a], at(dx=2))
        for d in (1, 3):
            remote(piece, piece, xas.at[kind(s)], xar.at[s, a], at(dx=d))

    def gate_up(s):
        return tuple(part_own[s][a, x] + zr[s][a].astype(F32) for a in range(2))

    def forward(s):
        settle(z4r.at[s, 0], zr[s].at[pl.ds(0, 2)])
        gate, up = gate_up(s)
        spread(s, 0, gate * jax.nn.sigmoid(gate) * up)

    def backward(s):
        settle(z4r.at[s, 1], zr[s].at[2])
        gate, up = gate_up(s)
        sig = jax.nn.sigmoid(gate)
        d_hidden = part_own[s][2, x] + zr[s][2].astype(F32)
        spread(s, 1, d_hidden * up * sig * (1.0 + gate * (1.0 - sig)))
        spread(s, 2, d_hidden * gate * sig)

    def relay(s, a):
        settle(xar.at[s, a], hid[s].at[a, k, pl.ds(0, 2)])
        if s in SMALL:
            piece = hid[s].at[a, k, (x + 4 - turn) % 4]
            remote(piece, piece, xas.at[0], xbr.at[s, a], at(dx=turn))
            return
        for i, d in enumerate((1, 3)):
            piece = hid[s].at[a, k, (x + 4 - d) % 4, pl.ds(16 * i, 16)]
            remote(piece, piece, xas.at[1], xbr.at[s, a], at(dx=d))

    def forward_hidden(s, a):
        if s in WHOLE:
            settle(xar.at[s, a], hid[s].at[a, k, pl.ds(0, 2)])
        settle(xbr.at[s, a], hid[s].at[a, k, (x + 2) % 4])
        remote(hid[s].at[a, k], hid[s].at[a, k], hfs.at[kind(s)], hfr.at[s, a], at(dk=1))

    def take(s, a):
        settle(hfr.at[s, a], hid[s].at[a, 1 - k])

    def project(s, b, other_core):
        n = len(STRIPS[s])
        kk = 1 - k if other_core else k
        if b == 0:
            res = dot(hid[s][0, kk].reshape(32 * n, 896), wd[0], ((1,), (0,)))
        else:
            res = (dot(hid[s][1, kk].reshape(32 * n, 896), wg[0], ((1,), (1,)))
                   + dot(hid[s][2, kk].reshape(32 * n, 896), wu[0], ((1,), (1,))))
        res = res.reshape(n, 32, 384)
        for i, (dy, j) in enumerate(STRIPS[s]):
            oparts_own[j, b, kk, (y + dy) % 4] = res[i]
            if dy:
                oparts[j, b, kk, (y + dy) % 4] = res[i].astype(BF16)
                remote(
                    oparts.at[j, b, kk, (y + dy) % 4], rs_y.at[j, b, dy - 1, kk],
                    yrs, yrr.at[j, b], at(dy=dy),
                )

    def grads(s, i):
        n = len(STRIPS[s])

        def rows(tc):
            return jnp.concatenate(
                [panel[j, tc, kk, (y + dy) % 4].reshape(32, 384) for kk in range(2) for dy, j in STRIPS[s]]
            )

        def units(a):
            return hid[s][a].reshape(64 * n, 896)

        if i < 2:
            acc, term = (gg, gu)[i], dot(rows(0), units(1 + i), ((0,), (0,)))
        else:
            acc, term = gd, dot(units(0), rows(1), ((0,), (0,)))
        if s > 0:
            term = acc[...] + term
        if s == STAGES - 1:
            term = term * scale
        acc[...] = term

    def sums(j):
        return (zout_b, rs_z_b, 0, zrs.at[1]) if j == 2 else (zout, rs_z, j, zrs.at[0])

    def sum_y(j, b):
        settle(yrr.at[j, b], rs_y.at[j, b])
        total = oparts_own[j, b, :, y]
        for d in (1, 2, 3):
            total = total + rs_y[j, b, d - 1].astype(F32)
        oparts_own[j, b, :, y] = total
        mine, theirs, i, ssem = sums(j)
        mine[i, b] = total.astype(mine.dtype).reshape(4, 16, 384)
        for d in (2, 1, 3):
            remote(mine.at[i, b, (zl + d) % 4], theirs.at[i, b, d - 1], ssem, zrr.at[j, b], at(dz=d))

    def finish(j, b):
        mine, theirs, i, ssem = sums(j)
        settle(zrr.at[j, b], theirs.at[i, b])
        total = oparts_own[j, b, zl // 2, y, pl.ds(pl.multiple_of(zl % 2 * 16, 16), 16)]
        for d in (1, 2, 3):
            total = total + theirs[i, b, d - 1].astype(F32)
        (out_ref, gin_ref)[b][pl.ds(16 * j, 16)] = total.astype(BF16)

    steps = (
        (send_z, 0, 0), (send_near, 0, 0), (send_z, 0, 1), (own_tiles,), (send_z, 1, 0), (send_near, 1, 0),
        (send_weights,), (gather_near, 0), (forward_core, 0, 0), (gather_near, 1), (partial, 0, 0), (send_z, 1, 1),
        (forward_core, 0, 1), (partial, 0, 1), (take_last, 0), (gather_mid, 0), (partial, 0, 2), (forward_core, 1, 0),
        (gather_end, 0), (take_last, 1), (partial, 1, 0), (sum_x, 0, 1), (forward_core, 1, 1), (partial, 1, 1),
        (gather_mid, 1), (sum_x, 0, 2), (forward_core, 2, 0), (sum_x, 0, 0), (pass_on, 1, 0), (partial, 1, 2),
        (pass_on, 1, 1), (partial, 2, 0), (gather_end, 1), (partial, 2, 1), (forward_core, 3, 0), (sum_x, 1, 0),
        (forward_core, 2, 1), (pass_on, 1, 2), (partial, 3, 0), (sum_x, 1, 1), (pass_on, 2, 0), (partial, 3, 1),
        (partial, 2, 2), (forward, 0), (sum_x, 1, 2), (pass_on, 2, 1), (pass_on, 3, 1), (sum_x, 2, 0),
        (forward_core, 3, 1), (pass_on, 3, 0), (pass_on, 2, 2), (backward, 0), (sum_x, 2, 1), (forward_hidden, 0, 0),
        (forward, 1), (partial, 3, 2), (sum_x, 2, 2), (backward, 1), (project, 0, 0, 0), (relay, 1, 0),
        (forward_hidden, 0, 2), (sum_x, 3, 0), (pass_on, 3, 2), (forward_hidden, 0, 1), (sum_x, 3, 1), (take, 0, 2),
        (relay, 1, 1), (forward, 2), (relay, 1, 2), (take, 0, 0), (project, 0, 1, 0), (forward_hidden, 1, 0),
        (sum_x, 3, 2), (grads, 0, 2), (backward, 2), (forward_hidden, 1, 1), (project, 1, 0, 0), (take, 1, 0),
        (relay, 2, 0), (project, 1, 0, 1), (forward_hidden, 1, 2), (forward, 3), (project, 1, 1, 0),
        (project, 0, 0, 1), (relay, 2, 1), (take, 1, 2), (take, 1, 1), (project, 1, 1, 1), (relay, 2, 2),
        (backward, 3), (forward_hidden, 2, 0), (project, 2, 0, 0), (sum_y, 0, 0), (grads, 0, 1), (grads, 1, 2),
        (forward_hidden, 3, 0), (take, 2, 0), (forward_hidden, 2, 1), (project, 2, 0, 1), (forward_hidden, 2, 2),
        (take, 0, 1), (project, 2, 1, 0), (grads, 2, 2), (project, 0, 1, 1), (grads, 1, 1), (take, 2, 2),
        (take, 2, 1), (take, 3, 0), (project, 2, 1, 1), (sum_y, 0, 1), (forward_hidden, 3, 1), (forward_hidden, 3, 2),
        (project, 3, 0, 0), (grads, 0, 0), (project, 3, 0, 1), (grads, 2, 1), (sum_y, 1, 0), (take, 3, 1),
        (take, 3, 2), (project, 3, 1, 0), (project, 3, 1, 1), (grads, 3, 2), (grads, 1, 0), (sum_y, 1, 1),
        (grads, 3, 1), (sum_y, 2, 0), (grads, 2, 0), (sum_y, 2, 1), (grads, 3, 0), (finish, 0, 0), (finish, 0, 1),
        (finish, 1, 0), (finish, 1, 1), (finish, 2, 0), (finish, 2, 1),
    )
    for step, *where in steps:
        step(*where)
    for i, ref in enumerate((wg, wu, wd)):
        settle(wsend.at[i], ref.at[1])
    settle(azs, other.at[:, :, pl.ds(0, 3), 0])
    settle(ats, other.at[:, :, :, 0])
    settle(ays.at[0], other.at[pl.ds(0, 2)])
    settle(ays.at[1], other.at[0])
    settle(afs, other)
    for i, ref in enumerate((part_s, part_l)):
        settle(xrs.at[i], ref.at[:, :, pl.ds(0, 3)])
        settle(xas.at[i], ref.at[:, :, pl.ds(0, 3)])
        settle(hfs.at[i], ref)
        settle(z4s.at[i], (zs_s, zs_l)[i])
        settle(zrs.at[i], (rs_z, rs_z_b)[i])
    settle(yrs, rs_y)


def write_out(*refs):
    copies = [pltpu.make_async_copy(refs[i], refs[5 + i], refs[10].at[i]) for i in range(5)]
    for copy in copies:
        copy.start()
    for copy in copies:
        copy.wait()


def body(tokens, gate_weight, up_weight, down_weight, cotangent):
    total_tokens = tokens.shape[0] * lax.axis_size("col")
    scale = total_tokens ** (-0.5)
    vmem = pl.BlockSpec(memory_space=pltpu.VMEM)
    hbm = pl.BlockSpec(memory_space=pl.ANY)
    sem = pltpu.SemaphoreType.DMA
    both = lambda *shape, dtype=BF16: [pltpu.VMEM((2, 3, *shape, r, 896), dtype) for r in (16, 32)]
    scratch = [
        pltpu.VMEM((TILES, 2, 2, 4, 2, 16, 384), BF16),
        pltpu.VMEM((TILES, 2, 4, 2, 16, 384), BF16),
        pltpu.VMEM((2, 384, 896), BF16),
        pltpu.VMEM((2, 384, 896), BF16),
        pltpu.VMEM((2, 896, 384), BF16),
        *both(4), *both(4, dtype=F32),
        pltpu.VMEM((2, 3, 1, 16, 896), BF16),
        pltpu.VMEM((2, 3, 2, 16, 896), BF16),
        *both(2), *both(), *both(), *both(2, 4),
        pltpu.VMEM((TILES, 2, 2, 4, 32, 384), BF16),
        pltpu.VMEM((TILES, 2, 2, 4, 32, 384), F32),
        pltpu.VMEM((TILES, 2, 3, 2, 32, 384), BF16),
        pltpu.VMEM((2, 2, 4, 16, 384), F32),
        pltpu.VMEM((1, 2, 4, 16, 384), BF16),
        pltpu.VMEM((2, 2, 3, 16, 384), F32),
        pltpu.VMEM((1, 2, 3, 16, 384), BF16),
        sem((4,)), sem((3,)), sem((3,)),
        sem(()), sem((2, 3)), sem((2,)), sem(()), sem((2,)), sem((2,)), sem((2,)), sem((2,)), sem(()), sem((STAGES, 2)),
        sem((2,)), sem((STAGES, 3)), sem((STAGES, 3)), sem((2,)), sem((STAGES, 2)),
        sem((2,)), sem((STAGES, 3)), sem((STAGES, 3)), sem((2,)), sem((STAGES, 3)),
        sem(()), sem((TILES, 2)), sem((2,)), sem((TILES, 2)),
    ]
    results = pl.pallas_call(
        functools.partial(kernel, scale),
        out_shape=(
            pltpu.VMEM((48, 384), BF16),
            pltpu.VMEM((48, 384), BF16),
            pltpu.VMEM((384, 896), F32),
            pltpu.VMEM((384, 896), F32),
            pltpu.VMEM((896, 384), F32),
        ),
        in_specs=[pl.BlockSpec(memory_space=pltpu.HBM)] * 5,
        out_specs=(vmem,) * 5,
        scratch_shapes=scratch,
        compiler_params=pltpu.CompilerParams(
            collective_id=0, has_side_effects=True, vmem_limit_bytes=36 * 1024 * 1024,
        ),
        cost_estimate=pl.CostEstimate(
            flops=2 * 9 * 768 * 384 * 896, bytes_accessed=8 * 1024 * 1024, transcendentals=0,
        ),
        name="ffn",
    )(*(
        pltpu.with_memory_space_constraint(a, pltpu.HBM)
        for a in (tokens.reshape(TILES, 16, 384), gate_weight, up_weight, down_weight,
                  cotangent.reshape(TILES, 16, 384))
    ))
    return pl.pallas_call(
        write_out,
        out_shape=tuple(jax.ShapeDtypeStruct(r.shape, r.dtype) for r in results),
        in_specs=[vmem] * 5,
        out_specs=(hbm,) * 5,
        scratch_shapes=[sem((5,))],
        compiler_params=pltpu.CompilerParams(vmem_limit_bytes=1024 * 1024),
        name="write_out",
    )(*results)


def solution(mesh):
    return jax.shard_map(
        body,
        mesh=mesh,
        in_specs=(
            P("col", "row"),
            P("row", "col"),
            P("row", "col"),
            P("col", "row"),
            P("col", "row"),
        ),
        out_specs=(
            P("col", "row"),
            P("col", "row"),
            P("row", "col"),
            P("row", "col"),
            P("col", "row"),
        ),
        check_vma=False,
    )
```

```python
import functools

import jax
import jax.numpy as jnp
from jax import lax
from jax.experimental import pallas as pl
from jax.experimental.pallas import tpu as pltpu
from jax.sharding import PartitionSpec as P

TILES = 3
STRAIGHT = (0,)
WHOLE = (0, 3)
BF16 = jnp.bfloat16
F32 = jnp.float32


def dot(a, b, dims):
    return lax.dot_general(a, b, (dims, ((), ())), preferred_element_type=F32)


STRIPS = (
    ((0, 0), (0, 1)),
    ((1, 0), (3, 0), (2, 0), (0, 2)),
    ((1, 1), (3, 1), (2, 1), (2, 2)),
    ((1, 2), (3, 2)),
)
STAGES = len(STRIPS)
SMALL = (0, 3)


def kernel(
    scale,
    tok_in, wg_in, wu_in, wd_in, cot_in,
    out_ref, gin_ref, gg, gu, gd,
    panel, other, wg, wu, wd,
    part_s, part_l, own_s, own_l, pairs_s, pairs_l, rs_x_s, rs_x_l, zs_s, zs_l, zr_s, zr_l, hid_s, hid_l,
    oparts, oparts_own, rs_y, zout, zout_b, rs_z, rs_z_b,
    load_sem, wsend, wrecv,
    azs, azr, azr_b, ats, atr, ays, ayr, ayr_b, afs, afr,
    xrs, xpr, xrr, z4s, z4r, xas, xar, xbr, hfs, hfr,
    yrs, yrr, zrs, zrr,
):
    row = lax.axis_index("row")
    col = lax.axis_index("col")
    x = row // 4
    zh = (row // 2) % 2
    k = row % 2
    y = col // 4
    zl = col % 4
    turn = 1 + 2 * k

    def at(dx=0, dz4=0, dk=0, dy=0, dz=0):
        xx = (x + dx) % 4
        zz = (zh + dz4) % 2
        kk = (k + dk) % 2
        yy = (y + dy) % 4
        ll = (zl + dz) % 4
        return {"row": xx * 4 + zz * 2 + kk, "col": yy * 4 + ll}

    def pick(s, small, large):
        return small.at[SMALL.index(s)] if s in SMALL else large.at[s - 1]

    def kind(s):
        return 0 if s in SMALL else 1

    part = [pick(s, part_s, part_l) for s in range(STAGES)]
    part_own = [pick(s, own_s, own_l) for s in range(STAGES)]
    pairs = [pick(s, pairs_s, pairs_l) for s in range(STAGES)]
    rs_x = [pick(s, rs_x_s, rs_x_l) for s in range(STAGES)]
    zs = [pick(s, zs_s, zs_l) for s in range(STAGES)]
    zr = [pick(s, zr_s, zr_l) for s in range(STAGES)]
    hid = [pick(s, hid_s, hid_l) for s in range(STAGES)]

    def settle(sem, ref):
        pltpu.make_async_copy(ref, ref, sem).wait()

    def remote(src, dst, ssem, rsem, device):
        copy = pltpu.make_async_remote_copy(
            src_ref=src, dst_ref=dst, send_sem=ssem, recv_sem=rsem,
            device_id=device, device_id_type=pl.DeviceIdType.MESH,
        )
        copy.start()
        return copy

    ins = (tok_in, cot_in)
    first, last = pl.ds(0, 2), pl.ds(2, 1)
    for tc in range(2):
        pltpu.make_async_copy(ins[tc], panel.at[:, tc, zl // 2, y, zl % 2], load_sem.at[3]).start()
    loads = []
    for i, (src, dst) in enumerate(((wg_in, wg), (wu_in, wu), (wd_in, wd))):
        loads.append(pltpu.make_async_copy(src, dst.at[0], load_sem.at[i]))
        loads[-1].start()

    barrier = pltpu.get_barrier_semaphore()
    peers = [at(dk=1), at(dz4=1)]
    peers += [at(dx=d) for d in (1, 2, 3)]
    peers += [at(dy=d) for d in (1, 2, 3)]
    peers += [at(dz=d) for d in (1, 2, 3)]
    for peer in peers:
        pl.semaphore_signal(barrier, inc=1, device_id=peer, device_id_type=pl.DeviceIdType.MESH)
    pl.semaphore_wait(barrier, len(peers))

    def tiles(js, tc, t):
        ll = (zl - t + 4) % 4
        return panel.at[js, tc, ll // 2, y, ll % 2]

    def send_z(late, tc):
        js = last if late else first
        for d in (1, 3, 2):
            remote(
                ins[tc].at[js], tiles(js, tc, 0),
                azs, azr_b.at[tc] if late else azr.at[tc, d - 1], at(dz=d),
            )

    def send_near(tc, t):
        src = tiles(0, tc, t) if t else ins[tc].at[0]
        for d in (1, 3, 2):
            remote(src, tiles(0, tc, t), ats, atr.at[tc], at(dy=d))

    wx = []

    def send_weights():
        for i, (src, dst) in enumerate(((wg_in, wg), (wu_in, wu), (wd_in, wd))):
            wx.append(remote(src, dst.at[1], wsend.at[i], wrecv.at[i], at(dk=1)))

    def own_tiles():
        settle(load_sem.at[3], other.at[:, :, 0, 0])

    def gather_near(tc):
        for t in (1, 3, 2):
            settle(azr.at[tc, t - 1], tiles(first, tc, t))
            send_near(tc, t)

    def take_last(tc):
        settle(azr_b.at[tc], other.at[0, tc, pl.ds(0, 3), 0])

    def gather_mid(tc):
        for d, js in ((1, pl.ds(1, 1)), (3, pl.ds(1, 1)), (2, pl.ds(1, 2))):
            block = panel.at[js, tc, :, y]
            remote(block, block, ays.at[0], ayr.at[tc], at(dy=d))

    def gather_end(tc):
        block = panel.at[last, tc, :, y]
        for d in (1, 3):
            remote(block, block, ays.at[1], ayr_b.at[tc], at(dy=d))

    def forward_core(s, tc):
        if s == 1:
            settle(atr.at[tc], other.at[:, :, pl.ds(0, 2), 0])
        if s == 2:
            settle(ayr.at[tc], other.at[0])
        if s == 3:
            settle(ayr_b.at[tc], other.at[0, tc])
        for dy in sorted({dy for dy, _ in STRIPS[s]}):
            js = [j for d, j in STRIPS[s] if d == dy]
            js = pl.ds(js[0], len(js))
            yy = (y + dy) % 4
            remote(panel.at[js, tc, 1 - k, yy], other.at[js, tc, yy], afs, afr.at[s, tc], at(dk=1))

    def partial(s, a):
        tc = 0 if a < 2 else 1
        n = len(STRIPS[s])
        if a != 1:
            settle(afr.at[s, tc], other.at[0, tc, pl.ds(0, n)])
        if s == 0:
            loads[a].wait()
            wx[a].wait_recv()
        lhs0 = jnp.concatenate([panel[j, tc, k, (y + dy) % 4].reshape(32, 384) for dy, j in STRIPS[s]])
        lhs1 = jnp.concatenate([other[j, tc, (y + dy) % 4].reshape(32, 384) for dy, j in STRIPS[s]])
        w = (wg, wu, wd)[a]
        if a < 2:
            res = dot(lhs0, w[0], ((1,), (0,))) + dot(lhs1, w[1], ((1,), (0,)))
        else:
            res = dot(lhs0, w[0], ((1,), (1,))) + dot(lhs1, w[1], ((1,), (1,)))
        part_own[s][a] = res.reshape(4, 8 * n, 896)
        part[s][a] = res.astype(BF16).reshape(4, 8 * n, 896)
        ssem = xrs.at[kind(s)]
        if s in STRAIGHT:
            if s in SMALL:
                remote(part[s].at[a, (x + 2) % 4], pairs[s].at[a, 0], ssem, xpr.at[s, a], at(dx=2))
            else:
                for i in range(2):
                    remote(part[s].at[a, (x + 2) % 4, pl.ds(16 * i, 16)], pairs[s].at[a, i],
                           ssem, xpr.at[s, a], at(dx=2))
            for i, d in enumerate((1, 3)):
                remote(part[s].at[a, (x + d) % 4], rs_x[s].at[a, i], ssem, xrr.at[s, a], at(dx=d))
        elif s in SMALL:
            remote(part[s].at[a, (x + 2) % 4], pairs[s].at[a, 0], ssem, xpr.at[s, a], at(dx=turn))
            remote(part[s].at[a, (x + 4 - turn) % 4], rs_x[s].at[a, 1], ssem, xrr.at[s, a], at(dx=4 - turn))
        else:
            for i, d in enumerate((1, 3)):
                remote(part[s].at[a, (x + 2) % 4, pl.ds(16 * i, 16)], pairs[s].at[a, i],
                       ssem, xpr.at[s, a], at(dx=d))
            for i, d in enumerate((1, 3)):
                rows = pl.ds(16 - 16 * i, 16)
                remote(part[s].at[a, (x + d) % 4, rows], rs_x[s].at[a, i, rows], ssem, xrr.at[s, a], at(dx=d))

    def pass_on(s, a):
        ssem = xrs.at[kind(s)]
        settle(xpr.at[s, a], pairs[s].at[a])
        if s in SMALL:
            both = part_own[s][a, (x + turn) % 4] + pairs[s][a, 0].astype(F32)
            part[s][a, (x + turn) % 4] = both.astype(BF16)
            remote(part[s].at[a, (x + turn) % 4], rs_x[s].at[a, 0], ssem, xrr.at[s, a], at(dx=turn))
            return
        for i, d in enumerate((1, 3)):
            rows = pl.ds(16 * i, 16)
            both = part_own[s][a, (x + d) % 4, rows] + pairs[s][a, i].astype(F32)
            part[s][a, (x + d) % 4, rows] = both.astype(BF16)
            remote(part[s].at[a, (x + d) % 4, rows], rs_x[s].at[a, i, rows], ssem, xrr.at[s, a], at(dx=d))

    def sum_x(s, a):
        settle(xrr.at[s, a], rs_x[s].at[a])
        total = part_own[s][a, x] + rs_x[s][a, 0].astype(F32) + rs_x[s][a, 1].astype(F32)
        if s in STRAIGHT:
            settle(xpr.at[s, a], pairs[s].at[a])
            total = total + pairs[s][a].reshape(total.shape).astype(F32)
        part_own[s][a, x] = total
        zs[s][a] = total.astype(BF16)
        remote(zs[s].at[a], zr[s].at[a], z4s.at[kind(s)], z4r.at[s, a // 2], at(dz4=1))

    def spread(s, a, value):
        hid[s][a, k, x] = value.astype(BF16)
        piece = hid[s].at[a, k, x]
        if s in WHOLE:
            remote(piece, piece, xas.at[kind(s)], xbr.at[s, a], at(dx=2))
        for d in (1, 3):
            remote(piece, piece, xas.at[kind(s)], xar.at[s, a], at(dx=d))

    def gate_up(s):
        return tuple(part_own[s][a, x] + zr[s][a].astype(F32) for a in range(2))

    def forward(s):
        settle(z4r.at[s, 0], zr[s].at[pl.ds(0, 2)])
        gate, up = gate_up(s)
        spread(s, 0, gate * jax.nn.sigmoid(gate) * up)

    def backward(s):
        settle(z4r.at[s, 1], zr[s].at[2])
        gate, up = gate_up(s)
        sig = jax.nn.sigmoid(gate)
        d_hidden = part_own[s][2, x] + zr[s][2].astype(F32)
        spread(s, 1, d_hidden * up * sig * (1.0 + gate * (1.0 - sig)))
        spread(s, 2, d_hidden * gate * sig)

    def relay(s, a):
        settle(xar.at[s, a], hid[s].at[a, k, pl.ds(0, 2)])
        if s in SMALL:
            piece = hid[s].at[a, k, (x + 4 - turn) % 4]
            remote(piece, piece, xas.at[0], xbr.at[s, a], at(dx=turn))
            return
        for i, d in enumerate((1, 3)):
            piece = hid[s].at[a, k, (x + 4 - d) % 4, pl.ds(16 * i, 16)]
            remote(piece, piece, xas.at[1], xbr.at[s, a], at(dx=d))

    def forward_hidden(s, a):
        if s in WHOLE:
            settle(xar.at[s, a], hid[s].at[a, k, pl.ds(0, 2)])
        settle(xbr.at[s, a], hid[s].at[a, k, (x + 2) % 4])
        remote(hid[s].at[a, k], hid[s].at[a, k], hfs.at[kind(s)], hfr.at[s, a], at(dk=1))

    def take(s, a):
        settle(hfr.at[s, a], hid[s].at[a, 1 - k])

    def project(s, b, other_core):
        n = len(STRIPS[s])
        kk = 1 - k if other_core else k
        if b == 0:
            res = dot(hid[s][0, kk].reshape(32 * n, 896), wd[0], ((1,), (0,)))
        else:
            res = (dot(hid[s][1, kk].reshape(32 * n, 896), wg[0], ((1,), (1,)))
                   + dot(hid[s][2, kk].reshape(32 * n, 896), wu[0], ((1,), (1,))))
        res = res.reshape(n, 32, 384)
        for i, (dy, j) in enumerate(STRIPS[s]):
            oparts_own[j, b, kk, (y + dy) % 4] = res[i]
            if dy:
                oparts[j, b, kk, (y + dy) % 4] = res[i].astype(BF16)
                remote(
                    oparts.at[j, b, kk, (y + dy) % 4], rs_y.at[j, b, dy - 1, kk],
                    yrs, yrr.at[j, b], at(dy=dy),
                )

    def grads(s, i):
        n = len(STRIPS[s])

        def rows(tc):
            return jnp.concatenate(
                [panel[j, tc, kk, (y + dy) % 4].reshape(32, 384) for kk in range(2) for dy, j in STRIPS[s]]
            )

        def units(a):
            return hid[s][a].reshape(64 * n, 896)

        if i < 2:
            acc, term = (gg, gu)[i], dot(rows(0), units(1 + i), ((0,), (0,)))
        else:
            acc, term = gd, dot(units(0), rows(1), ((0,), (0,)))
        if s > 0:
            term = acc[...] + term
        if s == STAGES - 1:
            term = term * scale
        acc[...] = term

    def sums(j):
        return (zout_b, rs_z_b, 0, zrs.at[1]) if j == 2 else (zout, rs_z, j, zrs.at[0])

    def sum_y(j, b):
        settle(yrr.at[j, b], rs_y.at[j, b])
        total = oparts_own[j, b, :, y]
        for d in (1, 2, 3):
            total = total + rs_y[j, b, d - 1].astype(F32)
        oparts_own[j, b, :, y] = total
        mine, theirs, i, ssem = sums(j)
        mine[i, b] = total.astype(mine.dtype).reshape(4, 16, 384)
        for d in (2, 1, 3):
            remote(mine.at[i, b, (zl + d) % 4], theirs.at[i, b, d - 1], ssem, zrr.at[j, b], at(dz=d))

    def finish(j, b):
        mine, theirs, i, ssem = sums(j)
        settle(zrr.at[j, b], theirs.at[i, b])
        total = oparts_own[j, b, zl // 2, y, pl.ds(pl.multiple_of(zl % 2 * 16, 16), 16)]
        for d in (1, 2, 3):
            total = total + theirs[i, b, d - 1].astype(F32)
        (out_ref, gin_ref)[b][pl.ds(16 * j, 16)] = total.astype(BF16)

    steps = (
        (send_z, 0, 0), (send_near, 0, 0), (send_z, 0, 1), (own_tiles,), (send_z, 1, 0), (send_near, 1, 0),
        (send_weights,), (gather_near, 0), (forward_core, 0, 0), (gather_near, 1), (partial, 0, 0), (send_z, 1, 1),
        (forward_core, 0, 1), (partial, 0, 1), (take_last, 0), (gather_mid, 0), (partial, 0, 2), (forward_core, 1, 0),
        (gather_end, 0), (take_last, 1), (partial, 1, 0), (sum_x, 0, 1), (forward_core, 1, 1), (partial, 1, 1),
        (gather_mid, 1), (sum_x, 0, 2), (forward_core, 2, 0), (sum_x, 0, 0), (pass_on, 1, 0), (partial, 1, 2),
        (pass_on, 1, 1), (partial, 2, 0), (gather_end, 1), (partial, 2, 1), (forward_core, 3, 0), (sum_x, 1, 0),
        (forward_core, 2, 1), (pass_on, 1, 2), (partial, 3, 0), (sum_x, 1, 1), (pass_on, 2, 0), (partial, 3, 1),
        (partial, 2, 2), (forward, 0), (sum_x, 1, 2), (pass_on, 2, 1), (pass_on, 3, 1), (sum_x, 2, 0),
        (forward_core, 3, 1), (pass_on, 3, 0), (pass_on, 2, 2), (backward, 0), (sum_x, 2, 1), (forward_hidden, 0, 0),
        (forward, 1), (partial, 3, 2), (sum_x, 2, 2), (backward, 1), (project, 0, 0, 0), (relay, 1, 0),
        (forward_hidden, 0, 2), (sum_x, 3, 0), (pass_on, 3, 2), (forward_hidden, 0, 1), (sum_x, 3, 1), (take, 0, 2),
        (relay, 1, 1), (forward, 2), (relay, 1, 2), (take, 0, 0), (project, 0, 1, 0), (forward_hidden, 1, 0),
        (sum_x, 3, 2), (grads, 0, 2), (backward, 2), (take, 0, 1), (project, 0, 1, 1), (forward_hidden, 1, 1),
        (project, 1, 0, 0), (take, 1, 0), (relay, 2, 0), (project, 1, 0, 1), (forward_hidden, 1, 2), (forward, 3),
        (project, 1, 1, 0), (project, 0, 0, 1), (relay, 2, 1), (take, 1, 2), (take, 1, 1), (project, 1, 1, 1),
        (relay, 2, 2), (backward, 3), (forward_hidden, 2, 0), (project, 2, 0, 0), (sum_y, 0, 0), (grads, 0, 1),
        (grads, 1, 2), (forward_hidden, 3, 0), (take, 2, 0), (forward_hidden, 2, 1), (project, 2, 0, 1),
        (forward_hidden, 2, 2), (project, 2, 1, 0), (take, 2, 2), (take, 2, 1), (take, 3, 0), (project, 2, 1, 1),
        (sum_y, 0, 1), (forward_hidden, 3, 1), (forward_hidden, 3, 2), (project, 3, 0, 0), (project, 3, 0, 1),
        (sum_y, 1, 0), (take, 3, 1), (take, 3, 2), (project, 3, 1, 0), (project, 3, 1, 1), (grads, 0, 0),
        (grads, 1, 0), (grads, 1, 1), (sum_y, 1, 1), (grads, 2, 0), (grads, 2, 1), (sum_y, 2, 0), (grads, 2, 2),
        (sum_y, 2, 1), (grads, 3, 0), (grads, 3, 1), (grads, 3, 2), (finish, 0, 0), (finish, 0, 1), (finish, 1, 0),
        (finish, 1, 1), (finish, 2, 0), (finish, 2, 1),
    )
    for step, *where in steps:
        step(*where)
    for i, ref in enumerate((wg, wu, wd)):
        settle(wsend.at[i], ref.at[1])
    settle(azs, other.at[:, :, pl.ds(0, 3), 0])
    settle(ats, other.at[:, :, :, 0])
    settle(ays.at[0], other.at[pl.ds(0, 2)])
    settle(ays.at[1], other.at[0])
    settle(afs, other)
    for i, ref in enumerate((part_s, part_l)):
        settle(xrs.at[i], ref.at[:, :, pl.ds(0, 3)])
        settle(xas.at[i], ref.at[:, :, pl.ds(0, 3)])
        settle(hfs.at[i], ref)
        settle(z4s.at[i], (zs_s, zs_l)[i])
        settle(zrs.at[i], (rs_z, rs_z_b)[i])
    settle(yrs, rs_y)


def write_out(*refs):
    copies = [pltpu.make_async_copy(refs[i], refs[5 + i], refs[10].at[i]) for i in range(5)]
    for copy in copies:
        copy.start()
    for copy in copies:
        copy.wait()


def body(tokens, gate_weight, up_weight, down_weight, cotangent):
    total_tokens = tokens.shape[0] * lax.axis_size("col")
    scale = total_tokens ** (-0.5)
    vmem = pl.BlockSpec(memory_space=pltpu.VMEM)
    hbm = pl.BlockSpec(memory_space=pl.ANY)
    sem = pltpu.SemaphoreType.DMA
    both = lambda *shape, dtype=BF16: [pltpu.VMEM((2, 3, *shape, r, 896), dtype) for r in (16, 32)]
    scratch = [
        pltpu.VMEM((TILES, 2, 2, 4, 2, 16, 384), BF16),
        pltpu.VMEM((TILES, 2, 4, 2, 16, 384), BF16),
        pltpu.VMEM((2, 384, 896), BF16),
        pltpu.VMEM((2, 384, 896), BF16),
        pltpu.VMEM((2, 896, 384), BF16),
        *both(4), *both(4, dtype=F32),
        pltpu.VMEM((2, 3, 1, 16, 896), BF16),
        pltpu.VMEM((2, 3, 2, 16, 896), BF16),
        *both(2), *both(), *both(), *both(2, 4),
        pltpu.VMEM((TILES, 2, 2, 4, 32, 384), BF16),
        pltpu.VMEM((TILES, 2, 2, 4, 32, 384), F32),
        pltpu.VMEM((TILES, 2, 3, 2, 32, 384), BF16),
        pltpu.VMEM((2, 2, 4, 16, 384), F32),
        pltpu.VMEM((1, 2, 4, 16, 384), BF16),
        pltpu.VMEM((2, 2, 3, 16, 384), F32),
        pltpu.VMEM((1, 2, 3, 16, 384), BF16),
        sem((4,)), sem((3,)), sem((3,)),
        sem(()), sem((2, 3)), sem((2,)), sem(()), sem((2,)), sem((2,)), sem((2,)), sem((2,)), sem(()), sem((STAGES, 2)),
        sem((2,)), sem((STAGES, 3)), sem((STAGES, 3)), sem((2,)), sem((STAGES, 2)),
        sem((2,)), sem((STAGES, 3)), sem((STAGES, 3)), sem((2,)), sem((STAGES, 3)),
        sem(()), sem((TILES, 2)), sem((2,)), sem((TILES, 2)),
    ]
    results = pl.pallas_call(
        functools.partial(kernel, scale),
        out_shape=(
            pltpu.VMEM((48, 384), BF16),
            pltpu.VMEM((48, 384), BF16),
            pltpu.VMEM((384, 896), F32),
            pltpu.VMEM((384, 896), F32),
            pltpu.VMEM((896, 384), F32),
        ),
        in_specs=[pl.BlockSpec(memory_space=pltpu.HBM)] * 5,
        out_specs=(vmem,) * 5,
        scratch_shapes=scratch,
        compiler_params=pltpu.CompilerParams(
            collective_id=0, has_side_effects=True, vmem_limit_bytes=36 * 1024 * 1024,
        ),
        cost_estimate=pl.CostEstimate(
            flops=2 * 9 * 768 * 384 * 896, bytes_accessed=8 * 1024 * 1024, transcendentals=0,
        ),
        name="ffn",
    )(*(
        pltpu.with_memory_space_constraint(a, pltpu.HBM)
        for a in (tokens.reshape(TILES, 16, 384), gate_weight, up_weight, down_weight,
                  cotangent.reshape(TILES, 16, 384))
    ))
    return pl.pallas_call(
        write_out,
        out_shape=tuple(jax.ShapeDtypeStruct(r.shape, r.dtype) for r in results),
        in_specs=[vmem] * 5,
        out_specs=(hbm,) * 5,
        scratch_shapes=[sem((5,))],
        compiler_params=pltpu.CompilerParams(vmem_limit_bytes=1024 * 1024),
        name="write_out",
    )(*results)


def solution(mesh):
    return jax.shard_map(
        body,
        mesh=mesh,
        in_specs=(
            P("col", "row"),
            P("row", "col"),
            P("row", "col"),
            P("col", "row"),
            P("col", "row"),
        ),
        out_specs=(
            P("col", "row"),
            P("col", "row"),
            P("row", "col"),
            P("row", "col"),
            P("col", "row"),
        ),
        check_vma=False,
    )
```

```python
import functools

import jax
import jax.numpy as jnp
from jax import lax
from jax.experimental import pallas as pl
from jax.experimental.pallas import tpu as pltpu
from jax.sharding import PartitionSpec as P

TILES = 3
STRAIGHT = (0,)
WHOLE = (0, 3)
BF16 = jnp.bfloat16
F32 = jnp.float32


def dot(a, b, dims):
    return lax.dot_general(a, b, (dims, ((), ())), preferred_element_type=F32)


STRIPS = (
    ((0, 0), (0, 1)),
    ((1, 0), (3, 0), (2, 0), (0, 2)),
    ((1, 1), (3, 1), (2, 1), (2, 2)),
    ((1, 2), (3, 2)),
)
STAGES = len(STRIPS)
SMALL = (0, 3)


def kernel(
    scale,
    tok_in, wg_in, wu_in, wd_in, cot_in,
    out_ref, gin_ref, gg, gu, gd,
    panel, other, wg, wu, wd,
    part_s, part_l, own_s, own_l, pairs_s, pairs_l, rs_x_s, rs_x_l, zs_s, zs_l, zr_s, zr_l, hid_s, hid_l,
    oparts, oparts_own, rs_y, zout, zout_b, rs_z, rs_z_b,
    load_sem, wsend, wrecv,
    azs, azr, azr_b, ats, atr, ays, ayr, ayr_b, afs, afr,
    xrs, xpr, xrr, z4s, z4r, xas, xar, xbr, hfs, hfr,
    yrs, yrr, zrs, zrr,
):
    row = lax.axis_index("row")
    col = lax.axis_index("col")
    x = row // 4
    zh = (row // 2) % 2
    k = row % 2
    y = col // 4
    zl = col % 4
    turn = 1 + 2 * k

    def at(dx=0, dz4=0, dk=0, dy=0, dz=0):
        xx = (x + dx) % 4
        zz = (zh + dz4) % 2
        kk = (k + dk) % 2
        yy = (y + dy) % 4
        ll = (zl + dz) % 4
        return {"row": xx * 4 + zz * 2 + kk, "col": yy * 4 + ll}

    def pick(s, small, large):
        return small.at[SMALL.index(s)] if s in SMALL else large.at[s - 1]

    def kind(s):
        return 0 if s in SMALL else 1

    part = [pick(s, part_s, part_l) for s in range(STAGES)]
    part_own = [pick(s, own_s, own_l) for s in range(STAGES)]
    pairs = [pick(s, pairs_s, pairs_l) for s in range(STAGES)]
    rs_x = [pick(s, rs_x_s, rs_x_l) for s in range(STAGES)]
    zs = [pick(s, zs_s, zs_l) for s in range(STAGES)]
    zr = [pick(s, zr_s, zr_l) for s in range(STAGES)]
    hid = [pick(s, hid_s, hid_l) for s in range(STAGES)]

    def settle(sem, ref):
        pltpu.make_async_copy(ref, ref, sem).wait()

    def remote(src, dst, ssem, rsem, device):
        copy = pltpu.make_async_remote_copy(
            src_ref=src, dst_ref=dst, send_sem=ssem, recv_sem=rsem,
            device_id=device, device_id_type=pl.DeviceIdType.MESH,
        )
        copy.start()
        return copy

    ins = (tok_in, cot_in)
    first, last = pl.ds(0, 2), pl.ds(2, 1)
    for tc in range(2):
        pltpu.make_async_copy(ins[tc], panel.at[:, tc, zl // 2, y, zl % 2], load_sem.at[3]).start()
    loads = []
    for i, (src, dst) in enumerate(((wg_in, wg), (wu_in, wu), (wd_in, wd))):
        loads.append(pltpu.make_async_copy(src, dst.at[0], load_sem.at[i]))
        loads[-1].start()

    barrier = pltpu.get_barrier_semaphore()
    peers = [at(dk=1), at(dz4=1)]
    peers += [at(dx=d) for d in (1, 2, 3)]
    peers += [at(dy=d) for d in (1, 2, 3)]
    peers += [at(dz=d) for d in (1, 2, 3)]
    for peer in peers:
        pl.semaphore_signal(barrier, inc=1, device_id=peer, device_id_type=pl.DeviceIdType.MESH)
    pl.semaphore_wait(barrier, len(peers))

    def tiles(js, tc, t):
        ll = (zl - t + 4) % 4
        return panel.at[js, tc, ll // 2, y, ll % 2]

    def send_z(late, tc):
        js = last if late else first
        for d in (1, 3, 2):
            remote(
                ins[tc].at[js], tiles(js, tc, 0),
                azs, azr_b.at[tc] if late else azr.at[tc, d - 1], at(dz=d),
            )

    def send_near(tc, t):
        src = tiles(0, tc, t) if t else ins[tc].at[0]
        for d in (1, 3, 2):
            remote(src, tiles(0, tc, t), ats, atr.at[tc], at(dy=d))

    wx = []

    def send_weights():
        for i, (src, dst) in enumerate(((wg_in, wg), (wu_in, wu), (wd_in, wd))):
            wx.append(remote(src, dst.at[1], wsend.at[i], wrecv.at[i], at(dk=1)))

    def own_tiles():
        settle(load_sem.at[3], other.at[:, :, 0, 0])

    def gather_near(tc):
        for t in (1, 3, 2):
            settle(azr.at[tc, t - 1], tiles(first, tc, t))
            send_near(tc, t)

    def take_last(tc):
        settle(azr_b.at[tc], other.at[0, tc, pl.ds(0, 3), 0])

    def gather_mid(tc):
        for d, js in ((1, pl.ds(1, 1)), (3, pl.ds(1, 1)), (2, pl.ds(1, 2))):
            block = panel.at[js, tc, :, y]
            remote(block, block, ays.at[0], ayr.at[tc], at(dy=d))

    def gather_end(tc):
        block = panel.at[last, tc, :, y]
        for d in (1, 3):
            remote(block, block, ays.at[1], ayr_b.at[tc], at(dy=d))

    def forward_core(s, tc):
        if s == 1:
            settle(atr.at[tc], other.at[:, :, pl.ds(0, 2), 0])
        if s == 2:
            settle(ayr.at[tc], other.at[0])
        if s == 3:
            settle(ayr_b.at[tc], other.at[0, tc])
        for dy in sorted({dy for dy, _ in STRIPS[s]}):
            js = [j for d, j in STRIPS[s] if d == dy]
            js = pl.ds(js[0], len(js))
            yy = (y + dy) % 4
            remote(panel.at[js, tc, 1 - k, yy], other.at[js, tc, yy], afs, afr.at[s, tc], at(dk=1))

    def partial(s, a):
        tc = 0 if a < 2 else 1
        n = len(STRIPS[s])
        if a != 1:
            settle(afr.at[s, tc], other.at[0, tc, pl.ds(0, n)])
        if s == 0:
            loads[a].wait()
            wx[a].wait_recv()
        lhs0 = jnp.concatenate([panel[j, tc, k, (y + dy) % 4].reshape(32, 384) for dy, j in STRIPS[s]])
        lhs1 = jnp.concatenate([other[j, tc, (y + dy) % 4].reshape(32, 384) for dy, j in STRIPS[s]])
        w = (wg, wu, wd)[a]
        if a < 2:
            res = dot(lhs0, w[0], ((1,), (0,))) + dot(lhs1, w[1], ((1,), (0,)))
        else:
            res = dot(lhs0, w[0], ((1,), (1,))) + dot(lhs1, w[1], ((1,), (1,)))
        part_own[s][a] = res.reshape(4, 8 * n, 896)
        part[s][a] = res.astype(BF16).reshape(4, 8 * n, 896)
        ssem = xrs.at[kind(s)]
        if s in STRAIGHT:
            if s in SMALL:
                remote(part[s].at[a, (x + 2) % 4], pairs[s].at[a, 0], ssem, xpr.at[s, a], at(dx=2))
            else:
                for i in range(2):
                    remote(part[s].at[a, (x + 2) % 4, pl.ds(16 * i, 16)], pairs[s].at[a, i],
                           ssem, xpr.at[s, a], at(dx=2))
            for i, d in enumerate((1, 3)):
                remote(part[s].at[a, (x + d) % 4], rs_x[s].at[a, i], ssem, xrr.at[s, a], at(dx=d))
        elif s in SMALL:
            remote(part[s].at[a, (x + 2) % 4], pairs[s].at[a, 0], ssem, xpr.at[s, a], at(dx=turn))
            remote(part[s].at[a, (x + 4 - turn) % 4], rs_x[s].at[a, 1], ssem, xrr.at[s, a], at(dx=4 - turn))
        else:
            for i, d in enumerate((1, 3)):
                remote(part[s].at[a, (x + 2) % 4, pl.ds(16 * i, 16)], pairs[s].at[a, i],
                       ssem, xpr.at[s, a], at(dx=d))
            for i, d in enumerate((1, 3)):
                rows = pl.ds(16 - 16 * i, 16)
                remote(part[s].at[a, (x + d) % 4, rows], rs_x[s].at[a, i, rows], ssem, xrr.at[s, a], at(dx=d))

    def pass_on(s, a):
        ssem = xrs.at[kind(s)]
        settle(xpr.at[s, a], pairs[s].at[a])
        if s in SMALL:
            both = part_own[s][a, (x + turn) % 4] + pairs[s][a, 0].astype(F32)
            part[s][a, (x + turn) % 4] = both.astype(BF16)
            remote(part[s].at[a, (x + turn) % 4], rs_x[s].at[a, 0], ssem, xrr.at[s, a], at(dx=turn))
            return
        for i, d in enumerate((1, 3)):
            rows = pl.ds(16 * i, 16)
            both = part_own[s][a, (x + d) % 4, rows] + pairs[s][a, i].astype(F32)
            part[s][a, (x + d) % 4, rows] = both.astype(BF16)
            remote(part[s].at[a, (x + d) % 4, rows], rs_x[s].at[a, i, rows], ssem, xrr.at[s, a], at(dx=d))

    def sum_x(s, a):
        settle(xrr.at[s, a], rs_x[s].at[a])
        total = part_own[s][a, x] + rs_x[s][a, 0].astype(F32) + rs_x[s][a, 1].astype(F32)
        if s in STRAIGHT:
            settle(xpr.at[s, a], pairs[s].at[a])
            total = total + pairs[s][a].reshape(total.shape).astype(F32)
        part_own[s][a, x] = total
        zs[s][a] = total.astype(BF16)
        remote(zs[s].at[a], zr[s].at[a], z4s.at[kind(s)], z4r.at[s, a // 2], at(dz4=1))

    def spread(s, a, value):
        hid[s][a, k, x] = value.astype(BF16)
        piece = hid[s].at[a, k, x]
        if s in WHOLE:
            remote(piece, piece, xas.at[kind(s)], xbr.at[s, a], at(dx=2))
        for d in (1, 3):
            remote(piece, piece, xas.at[kind(s)], xar.at[s, a], at(dx=d))

    def gate_up(s):
        return tuple(part_own[s][a, x] + zr[s][a].astype(F32) for a in range(2))

    def forward(s):
        settle(z4r.at[s, 0], zr[s].at[pl.ds(0, 2)])
        gate, up = gate_up(s)
        spread(s, 0, gate * jax.nn.sigmoid(gate) * up)

    def backward(s):
        settle(z4r.at[s, 1], zr[s].at[2])
        gate, up = gate_up(s)
        sig = jax.nn.sigmoid(gate)
        d_hidden = part_own[s][2, x] + zr[s][2].astype(F32)
        spread(s, 1, d_hidden * up * sig * (1.0 + gate * (1.0 - sig)))
        spread(s, 2, d_hidden * gate * sig)

    def relay(s, a):
        settle(xar.at[s, a], hid[s].at[a, k, pl.ds(0, 2)])
        if s in SMALL:
            piece = hid[s].at[a, k, (x + 4 - turn) % 4]
            remote(piece, piece, xas.at[0], xbr.at[s, a], at(dx=turn))
            return
        for i, d in enumerate((1, 3)):
            piece = hid[s].at[a, k, (x + 4 - d) % 4, pl.ds(16 * i, 16)]
            remote(piece, piece, xas.at[1], xbr.at[s, a], at(dx=d))

    def forward_hidden(s, a):
        if s in WHOLE:
            settle(xar.at[s, a], hid[s].at[a, k, pl.ds(0, 2)])
        settle(xbr.at[s, a], hid[s].at[a, k, (x + 2) % 4])
        remote(hid[s].at[a, k], hid[s].at[a, k], hfs.at[kind(s)], hfr.at[s, a], at(dk=1))

    def take(s, a):
        settle(hfr.at[s, a], hid[s].at[a, 1 - k])

    def project(s, b, other_core):
        n = len(STRIPS[s])
        kk = 1 - k if other_core else k
        if b == 0:
            res = dot(hid[s][0, kk].reshape(32 * n, 896), wd[0], ((1,), (0,)))
        else:
            res = (dot(hid[s][1, kk].reshape(32 * n, 896), wg[0], ((1,), (1,)))
                   + dot(hid[s][2, kk].reshape(32 * n, 896), wu[0], ((1,), (1,))))
        res = res.reshape(n, 32, 384)
        for i, (dy, j) in enumerate(STRIPS[s]):
            oparts_own[j, b, kk, (y + dy) % 4] = res[i]
            if dy:
                oparts[j, b, kk, (y + dy) % 4] = res[i].astype(BF16)
                remote(
                    oparts.at[j, b, kk, (y + dy) % 4], rs_y.at[j, b, dy - 1, kk],
                    yrs, yrr.at[j, b], at(dy=dy),
                )

    def grads(s, i):
        n = len(STRIPS[s])

        def rows(tc):
            return jnp.concatenate(
                [panel[j, tc, kk, (y + dy) % 4].reshape(32, 384) for kk in range(2) for dy, j in STRIPS[s]]
            )

        def units(a):
            return hid[s][a].reshape(64 * n, 896)

        if i < 2:
            acc, term = (gg, gu)[i], dot(rows(0), units(1 + i), ((0,), (0,)))
        else:
            acc, term = gd, dot(units(0), rows(1), ((0,), (0,)))
        if s > 0:
            term = acc[...] + term
        if s == STAGES - 1:
            term = term * scale
        acc[...] = term

    def sums(j):
        return (zout_b, rs_z_b, 0, zrs.at[1]) if j == 2 else (zout, rs_z, j, zrs.at[0])

    def sum_y(j, b):
        settle(yrr.at[j, b], rs_y.at[j, b])
        total = oparts_own[j, b, :, y]
        for d in (1, 2, 3):
            total = total + rs_y[j, b, d - 1].astype(F32)
        oparts_own[j, b, :, y] = total
        mine, theirs, i, ssem = sums(j)
        mine[i, b] = total.astype(mine.dtype).reshape(4, 16, 384)
        for d in (2, 1, 3):
            remote(mine.at[i, b, (zl + d) % 4], theirs.at[i, b, d - 1], ssem, zrr.at[j, b], at(dz=d))

    def finish(j, b):
        mine, theirs, i, ssem = sums(j)
        settle(zrr.at[j, b], theirs.at[i, b])
        total = oparts_own[j, b, zl // 2, y, pl.ds(pl.multiple_of(zl % 2 * 16, 16), 16)]
        for d in (1, 2, 3):
            total = total + theirs[i, b, d - 1].astype(F32)
        (out_ref, gin_ref)[b][pl.ds(16 * j, 16)] = total.astype(BF16)

    steps = (
        (send_z, 0, 0), (send_near, 0, 0), (send_z, 0, 1), (own_tiles,), (send_z, 1, 0), (send_near, 1, 0),
        (send_weights,), (gather_near, 0), (forward_core, 0, 0), (gather_near, 1), (partial, 0, 0), (send_z, 1, 1),
        (forward_core, 0, 1), (partial, 0, 1), (take_last, 0), (gather_mid, 0), (partial, 0, 2), (forward_core, 1, 0),
        (gather_end, 0), (take_last, 1), (partial, 1, 0), (sum_x, 0, 1), (forward_core, 1, 1), (partial, 1, 1),
        (gather_mid, 1), (sum_x, 0, 2), (forward_core, 2, 0), (sum_x, 0, 0), (pass_on, 1, 0), (partial, 1, 2),
        (pass_on, 1, 1), (partial, 2, 0), (gather_end, 1), (partial, 2, 1), (forward_core, 3, 0), (sum_x, 1, 0),
        (forward_core, 2, 1), (pass_on, 1, 2), (partial, 3, 0), (sum_x, 1, 1), (pass_on, 2, 0), (partial, 3, 1),
        (partial, 2, 2), (forward, 0), (sum_x, 1, 2), (pass_on, 2, 1), (pass_on, 3, 1), (sum_x, 2, 0),
        (forward_core, 3, 1), (pass_on, 3, 0), (pass_on, 2, 2), (backward, 0), (sum_x, 2, 1), (forward_hidden, 0, 0),
        (forward, 1), (partial, 3, 2), (sum_x, 2, 2), (backward, 1), (project, 0, 0, 0), (relay, 1, 0),
        (forward_hidden, 0, 2), (sum_x, 3, 0), (pass_on, 3, 2), (forward_hidden, 0, 1), (sum_x, 3, 1), (take, 0, 2),
        (relay, 1, 1), (forward, 2), (relay, 1, 2), (take, 0, 0), (project, 0, 1, 0), (forward_hidden, 1, 0),
        (sum_x, 3, 2), (grads, 0, 2), (backward, 2), (forward_hidden, 1, 1), (project, 1, 0, 0), (take, 1, 0),
        (relay, 2, 0), (project, 1, 0, 1), (forward_hidden, 1, 2), (forward, 3), (project, 1, 1, 0),
        (project, 0, 0, 1), (relay, 2, 1), (take, 1, 2), (take, 1, 1), (project, 1, 1, 1), (relay, 2, 2),
        (backward, 3), (forward_hidden, 2, 0), (project, 2, 0, 0), (sum_y, 0, 0), (grads, 0, 1), (grads, 1, 2),
        (forward_hidden, 3, 0), (take, 2, 0), (forward_hidden, 2, 1), (project, 2, 0, 1), (forward_hidden, 2, 2),
        (take, 0, 1), (project, 2, 1, 0), (grads, 2, 2), (project, 0, 1, 1), (grads, 1, 1), (take, 2, 2),
        (take, 2, 1), (take, 3, 0), (forward_hidden, 3, 1), (forward_hidden, 3, 2), (project, 2, 1, 1), (sum_y, 0, 1),
        (project, 3, 0, 0), (grads, 0, 0), (project, 3, 0, 1), (grads, 2, 1), (sum_y, 1, 0), (take, 3, 1),
        (take, 3, 2), (project, 3, 1, 0), (project, 3, 1, 1), (grads, 3, 2), (grads, 1, 0), (sum_y, 1, 1),
        (grads, 3, 1), (sum_y, 2, 0), (grads, 2, 0), (sum_y, 2, 1), (grads, 3, 0), (finish, 0, 0), (finish, 0, 1),
        (finish, 1, 0), (finish, 1, 1), (finish, 2, 0), (finish, 2, 1),
    )
    for step, *where in steps:
        step(*where)
    for i, ref in enumerate((wg, wu, wd)):
        settle(wsend.at[i], ref.at[1])
    settle(azs, other.at[:, :, pl.ds(0, 3), 0])
    settle(ats, other.at[:, :, :, 0])
    settle(ays.at[0], other.at[pl.ds(0, 2)])
    settle(ays.at[1], other.at[0])
    settle(afs, other)
    for i, ref in enumerate((part_s, part_l)):
        settle(xrs.at[i], ref.at[:, :, pl.ds(0, 3)])
        settle(xas.at[i], ref.at[:, :, pl.ds(0, 3)])
        settle(hfs.at[i], ref)
        settle(z4s.at[i], (zs_s, zs_l)[i])
        settle(zrs.at[i], (rs_z, rs_z_b)[i])
    settle(yrs, rs_y)


def write_out(*refs):
    copies = [pltpu.make_async_copy(refs[i], refs[5 + i], refs[10].at[i]) for i in range(5)]
    for copy in copies:
        copy.start()
    for copy in copies:
        copy.wait()


def body(tokens, gate_weight, up_weight, down_weight, cotangent):
    total_tokens = tokens.shape[0] * lax.axis_size("col")
    scale = total_tokens ** (-0.5)
    vmem = pl.BlockSpec(memory_space=pltpu.VMEM)
    hbm = pl.BlockSpec(memory_space=pl.ANY)
    sem = pltpu.SemaphoreType.DMA
    both = lambda *shape, dtype=BF16: [pltpu.VMEM((2, 3, *shape, r, 896), dtype) for r in (16, 32)]
    scratch = [
        pltpu.VMEM((TILES, 2, 2, 4, 2, 16, 384), BF16),
        pltpu.VMEM((TILES, 2, 4, 2, 16, 384), BF16),
        pltpu.VMEM((2, 384, 896), BF16),
        pltpu.VMEM((2, 384, 896), BF16),
        pltpu.VMEM((2, 896, 384), BF16),
        *both(4), *both(4, dtype=F32),
        pltpu.VMEM((2, 3, 1, 16, 896), BF16),
        pltpu.VMEM((2, 3, 2, 16, 896), BF16),
        *both(2), *both(), *both(), *both(2, 4),
        pltpu.VMEM((TILES, 2, 2, 4, 32, 384), BF16),
        pltpu.VMEM((TILES, 2, 2, 4, 32, 384), F32),
        pltpu.VMEM((TILES, 2, 3, 2, 32, 384), BF16),
        pltpu.VMEM((2, 2, 4, 16, 384), F32),
        pltpu.VMEM((1, 2, 4, 16, 384), BF16),
        pltpu.VMEM((2, 2, 3, 16, 384), F32),
        pltpu.VMEM((1, 2, 3, 16, 384), BF16),
        sem((4,)), sem((3,)), sem((3,)),
        sem(()), sem((2, 3)), sem((2,)), sem(()), sem((2,)), sem((2,)), sem((2,)), sem((2,)), sem(()), sem((STAGES, 2)),
        sem((2,)), sem((STAGES, 3)), sem((STAGES, 3)), sem((2,)), sem((STAGES, 2)),
        sem((2,)), sem((STAGES, 3)), sem((STAGES, 3)), sem((2,)), sem((STAGES, 3)),
        sem(()), sem((TILES, 2)), sem((2,)), sem((TILES, 2)),
    ]
    results = pl.pallas_call(
        functools.partial(kernel, scale),
        out_shape=(
            pltpu.VMEM((48, 384), BF16),
            pltpu.VMEM((48, 384), BF16),
            pltpu.VMEM((384, 896), F32),
            pltpu.VMEM((384, 896), F32),
            pltpu.VMEM((896, 384), F32),
        ),
        in_specs=[pl.BlockSpec(memory_space=pltpu.HBM)] * 5,
        out_specs=(vmem,) * 5,
        scratch_shapes=scratch,
        compiler_params=pltpu.CompilerParams(
            collective_id=0, has_side_effects=True, vmem_limit_bytes=36 * 1024 * 1024,
        ),
        cost_estimate=pl.CostEstimate(
            flops=2 * 9 * 768 * 384 * 896, bytes_accessed=8 * 1024 * 1024, transcendentals=0,
        ),
        name="ffn",
    )(*(
        pltpu.with_memory_space_constraint(a, pltpu.HBM)
        for a in (tokens.reshape(TILES, 16, 384), gate_weight, up_weight, down_weight,
                  cotangent.reshape(TILES, 16, 384))
    ))
    return pl.pallas_call(
        write_out,
        out_shape=tuple(jax.ShapeDtypeStruct(r.shape, r.dtype) for r in results),
        in_specs=[vmem] * 5,
        out_specs=(hbm,) * 5,
        scratch_shapes=[sem((5,))],
        compiler_params=pltpu.CompilerParams(vmem_limit_bytes=1024 * 1024),
        name="write_out",
    )(*results)


def solution(mesh):
    return jax.shard_map(
        body,
        mesh=mesh,
        in_specs=(
            P("col", "row"),
            P("row", "col"),
            P("row", "col"),
            P("col", "row"),
            P("col", "row"),
        ),
        out_specs=(
            P("col", "row"),
            P("col", "row"),
            P("row", "col"),
            P("row", "col"),
            P("col", "row"),
        ),
        check_vma=False,
    )
```
